32 devices in a mesh: group: 2 (over x), expert: 16 (over z, y, core).
Axes of the slice: x: 2, y: 2, z: 4, core: 2. Of those that a mesh axis runs over, the one named last changes fastest.
Arguments:
- hidden: bfloat16 [4096, 4096], P(('group', 'expert')), parts along dimension 0, may hold values from -6 to 6
- norm_gain: bfloat16 [4096], replicated, may hold values from 0.25 to 1.75
- router_weight: bfloat16 [4096, 128], replicated, may hold values from -0.03125 to 0.03125
- expert_ids: int32 [4096, 8], P(('group', 'expert')), parts along dimension 0, may hold values from 0 to 127, all different within a row; in each aligned block of 128 rows (0 to 127, 128 to 255, ...) at most 16 rows name the same one
- gate_weight: bfloat16 [16, 4096, 384], P('expert'), may hold values from -0.09375 to 0.09375
- up_weight: bfloat16 [16, 4096, 384], P('expert'), may hold values from -0.09375 to 0.09375
- down_weight: bfloat16 [16, 384, 4096], P('expert'), may hold values from -0.625 to 0.625
Outputs:
- moe_out: bfloat16 [4096, 4096], P(('group', 'expert')), parts along dimension 0
The draws below stay inside these ranges and needn't reach their ends.
There are 2 independent parts, one for each index of `group`. The reference program is written for one: setup_inputs(seed, part) draws one part's arguments, and reference() takes and returns one part's arrays. A program takes and returns all parts, laid end to end along the dimension named above; an argument that names none is the same for every part. Nothing has to cross between parts.
Inputs may be any that keep to these rules, and one draw needn't show every extreme that they name: `expert_ids`: each row names 8 different experts; in each aligned block of 128 rows (the rows of one device) no expert is named by more than 16 rows.
All inputs are finite; a program needn't handle non-finite values.
Results may differ from the reference program's by a relative error of at most 0.0077.
Values may be sent and summed in bfloat16 or wider, within the bound.
No kernel may reach another device: no remote copies, remote signals or barrier semaphores. Data moves between devices by JAX's collectives and lax.ppermute only.
A program may use at most 128 MiB of HBM per device.

```python
import math
import jax
import jax.numpy as jnp
import numpy as np
from jax import lax

D = 4096
FF = 1536
EXPERTS = 128
TOP = 8
TOK_DEV = 128
SPLIT = 4
SLICE = 384
E_FLIGHT = 4
CAP = 16
TOKENS = 2048
N_EXPERT = 16


def levels(stream_key, extent, pieces, least, largest):
    factor_of, own = 1.0, jax.random.fold_in(stream_key, 6)
    for position, blocks in pieces:
        steps = jnp.exp(jax.random.uniform(jax.random.fold_in(own, position), (blocks,), jnp.float32, least / len(pieces), largest / len(pieces)))
        factor_of = factor_of * jnp.repeat(steps, extent[position] // blocks).reshape([-1 if axis == position else 1 for axis in range(len(extent))])
    return factor_of


def shared_out(key, own, number, rows, count, top, reach, lean):
    ranking = jax.random.permutation(key, count)
    packed, usual = load_shares(count, rows * top, reach, lean, True), load_shares(count, rows * top, reach, lean, False)
    places = jnp.arange(count)

    def named(lengths, turn):
        used = int((lengths > 0).sum())
        fixed = max(1, used // 4)
        shifted = fixed + (places - fixed + turn * (used - fixed)) % max(1, count - fixed)
        return jnp.zeros((count,), jnp.int32).at[ranking[jnp.where(places < fixed, places, shifted)]].set(jnp.asarray(lengths, jnp.int32))

    lengths = jnp.where(number % 4 == 0, named(packed, number // 4), named(usual, number - number // 4 - 1))
    mixed = jax.random.permutation(jax.random.fold_in(own, 3), count)
    donor, sink = mixed[0:count // 2 * 2:2], mixed[1:count // 2 * 2:2]
    room = jnp.minimum(lengths[donor] - 1, reach - lengths[sink]) // 2
    room = jnp.where((donor == ranking[0]) | (sink == ranking[0]) | (lengths[sink] == 0), 0, jnp.maximum(room, 0))
    shifted = jax.random.randint(jax.random.fold_in(own, 4), (count // 2,), 0, 1 << 20) % (room + 1)
    lengths = lengths.at[donor].add(-shifted).at[sink].add(shifted)
    labels = jnp.searchsorted(jnp.cumsum(lengths), jnp.arange(rows * top), side="right").astype(jnp.int32)
    table = labels.reshape(top, rows).T
    table = table[jax.random.permutation(jax.random.fold_in(own, 1), rows)]
    turn = jax.random.randint(jax.random.fold_in(own, 2), (rows, 1), 0, top)
    return jnp.take_along_axis(table, (jnp.arange(top)[None, :] + turn) % top, axis=1)


def load_shares(number_of, total, most, skew, full):
    loads = [(1 << 20) // math.isqrt(rank ** skew) + 1 for rank in range(1, number_of + 1)]
    largest = most if full else min(most, max(-(-total // number_of), total * loads[0] // sum(loads)))
    least = 1 if total - largest >= number_of - 1 else 0
    holding, rest = [largest] + [least] * (number_of - 1), total - largest - least * (number_of - 1)
    while rest > 0:
        free = [i for i in range(1, number_of) if holding[i] < largest] or [i for i in range(1, number_of) if holding[i] < most]
        whole, remaining = sum([loads[i] for i in free]), rest
        for i in free:
            more = min(most - holding[i], max(1, remaining * loads[i] // whole), rest)
            holding[i] = holding[i] + more
            rest = rest - more
    return np.array(holding)


def noise(key, dims, width, limit, cuts=(), kind=jnp.bfloat16):
    drawn = jax.random.normal(key, dims, jnp.float32) * width
    if len(cuts) > 0:
        drawn = levels(key, dims, cuts, -0.22, 0.18) * drawn
    return jnp.clip(drawn, min=-limit, max=limit).astype(kind)


def setup_inputs(seed: int = 0, part: int = 0) -> dict:
    keys = jax.random.split(jax.random.key(seed), 8)
    part_splits = jax.random.split(jax.random.fold_in(keys[7], part), 8)
    hidden = noise(part_splits[0], (TOKENS, D), 1.0, 6.0, ((0, 16),))
    norm_gain = jnp.clip(1.0 + 0.15 * jax.random.normal(keys[1], (D,), jnp.float32), 0.25, 1.75).astype(jnp.bfloat16)
    router_weight = noise(keys[2], (D, EXPERTS), (8 * D) ** -0.5, 0.03125)
    expert_ids_keys = jax.random.split(jax.random.fold_in(part_splits[3], 1), TOKENS // TOK_DEV)
    expert_ids_turns = jax.random.permutation(jax.random.fold_in(part_splits[3], 3), TOKENS // TOK_DEV)
    expert_ids = jax.vmap(lambda own, number: shared_out(jax.random.fold_in(part_splits[3], 2), own, number, TOK_DEV, EXPERTS, TOP, CAP, 2))(expert_ids_keys, expert_ids_turns).reshape((TOKENS, TOP))
    gate_weight = noise(keys[4], (N_EXPERT, D, SLICE), D ** -0.5, 0.09375, ((0, 16),))
    up_weight = noise(keys[5], (N_EXPERT, D, SLICE), D ** -0.5, 0.09375, ((0, 16),))
    down_weight = noise(keys[6], (N_EXPERT, SLICE, D), (FF // 16) ** -0.5, 0.625, ((0, 16),))
    return {"hidden": hidden, "norm_gain": norm_gain, "router_weight": router_weight, "expert_ids": expert_ids, "gate_weight": gate_weight, "up_weight": up_weight, "down_weight": down_weight}


def reference(hidden, norm_gain, router_weight, expert_ids, gate_weight, up_weight, down_weight):
    widened = hidden.astype(jnp.float32)
    inv_rms = lax.rsqrt(lax.optimization_barrier(jnp.mean(widened * widened, axis=-1, keepdims=True)) + 1e-06)
    normed = (widened * inv_rms * norm_gain.astype(jnp.float32)).astype(jnp.bfloat16)
    logits = jnp.dot(normed, router_weight, preferred_element_type=jnp.float32)
    router_probs = jax.nn.softmax(logits, axis=-1)
    picked = jnp.take_along_axis(router_probs, expert_ids, axis=1)
    gate_share = picked / lax.optimization_barrier(jnp.sum(picked, axis=1, keepdims=True))

    def one_expert(expert, running):
        summed = jnp.zeros(hidden.shape, jnp.float32)
        for member in range(SPLIT):
            shard_row = member * E_FLIGHT + expert
            gate_mat = lax.dynamic_index_in_dim(gate_weight, shard_row, 0, keepdims=False)
            up_mat = lax.dynamic_index_in_dim(up_weight, shard_row, 0, keepdims=False)
            down_mat = lax.dynamic_index_in_dim(down_weight, shard_row, 0, keepdims=False)
            gate_act = jnp.dot(normed, gate_mat, preferred_element_type=jnp.float32)
            up_act = jnp.dot(normed, up_mat, preferred_element_type=jnp.float32)
            hidden_act = (jax.nn.silu(gate_act) * up_act).astype(jnp.bfloat16)
            partial_value = jnp.dot(hidden_act, down_mat, preferred_element_type=jnp.float32).astype(jnp.bfloat16)
            summed = summed + lax.optimization_barrier(partial_value).astype(jnp.float32)
        expert_out = lax.optimization_barrier(summed.astype(jnp.bfloat16)).astype(jnp.float32)
        weight = lax.optimization_barrier(jnp.sum(jnp.where(expert_ids == expert, gate_share, jnp.zeros_like(gate_share)), axis=1))
        return running + weight[:, None] * expert_out
    running = lax.fori_loop(0, E_FLIGHT, one_expert, jnp.zeros(hidden.shape, jnp.float32))
    return running.astype(jnp.bfloat16)
```

```python
import functools

import jax
import jax.numpy as jnp
from jax import lax
from jax.experimental import pallas as pl
from jax.experimental.pallas import tpu as pltpu
from jax.sharding import PartitionSpec as P

SPLIT = 4
CAP = 16
EPS = 1e-06


def slots_of(ids, flight):
    tokens = ids.shape[1]
    named = jnp.concatenate(
        [
            jnp.max((ids == e).astype(jnp.float32), axis=0, keepdims=True)
            for e in range(flight)
        ],
        axis=0,
    )
    earlier = lax.broadcasted_iota(jnp.int32, (tokens, tokens), 0) < lax.broadcasted_iota(
        jnp.int32, (tokens, tokens), 1
    )
    place = jnp.dot(
        named.astype(jnp.bfloat16),
        earlier.astype(jnp.float32).astype(jnp.bfloat16),
        preferred_element_type=jnp.float32,
    )
    return named, place


def spread(named, place, value, flight):
    slot = lax.broadcasted_iota(jnp.int32, (CAP, named.shape[1]), 0).astype(jnp.float32)
    return jnp.concatenate(
        [
            jnp.where(
                (place[e : e + 1] == slot) & (named[e : e + 1] > 0.0), value[e : e + 1], 0.0
            )
            for e in range(flight)
        ],
        axis=0,
    )


def inv_rms_of(hidden_ref):
    rows, width = hidden_ref.shape
    piece = min(width, 512)

    def add(i, total):
        x = hidden_ref[:, pl.ds(pl.multiple_of(i * piece, piece), piece)].astype(jnp.float32)
        return total + jnp.sum(x * x, axis=1, keepdims=True)

    total = lax.fori_loop(0, width // piece, add, jnp.zeros((rows, 1), jnp.float32), unroll=True)
    return lax.rsqrt(total / width + EPS)


def dispatch_kernel(flight, hidden_ref, gain_ref, ids_ref, out_ref):
    width = hidden_ref.shape[1]
    piece = min(width, 512)
    inv_rms = inv_rms_of(hidden_ref)
    named, place = slots_of(ids_ref[...], flight)
    select = spread(named, place, named, flight).astype(jnp.bfloat16)
    for i in range(width // piece):
        cols = pl.ds(i * piece, piece)
        x = hidden_ref[:, cols].astype(jnp.float32)
        normed = (x * inv_rms * gain_ref[:, cols].astype(jnp.float32)).astype(jnp.bfloat16)
        out_ref[:, cols] = jnp.dot(select, normed, preferred_element_type=jnp.float32).astype(
            jnp.bfloat16
        )


def shares_kernel(flight, hidden_ref, gain_ref, ids_ref, router_ref, out_ref):
    width = hidden_ref.shape[1]
    experts = router_ref.shape[1]
    piece = min(width, 512)
    inv_rms = inv_rms_of(hidden_ref)
    logits = jnp.zeros((hidden_ref.shape[0], experts), jnp.float32)
    for i in range(width // piece):
        cols = pl.ds(i * piece, piece)
        x = hidden_ref[:, cols].astype(jnp.float32)
        normed = (x * inv_rms * gain_ref[:, cols].astype(jnp.float32)).astype(jnp.bfloat16)
        logits += jnp.dot(normed, router_ref[cols, :], preferred_element_type=jnp.float32)
    logits = logits.T
    raised = jnp.exp(logits - jnp.max(logits, axis=0, keepdims=True))
    probs = raised / jnp.sum(raised, axis=0, keepdims=True)
    ids = ids_ref[...]
    expert = lax.broadcasted_iota(jnp.int32, probs.shape, 0)
    picked = jnp.zeros(probs.shape, jnp.float32)
    for k in range(ids.shape[0]):
        picked = jnp.where(ids[k : k + 1] == expert, probs, picked)
    share = probs[:flight] / jnp.sum(picked, axis=0, keepdims=True)
    named, place = slots_of(ids, flight)
    weight = spread(named, place, share, flight).T
    high = weight.astype(jnp.bfloat16)
    low = (weight - high.astype(jnp.float32)).astype(jnp.bfloat16)
    out_ref[...] = jnp.concatenate([high, low], axis=1)


def combine_kernel(weight_ref, *refs):
    *parts, out_ref = refs
    total = parts[0][...].astype(jnp.float32)
    for part in parts[1:]:
        total = total + part[...].astype(jnp.float32)
    rows = total.astype(jnp.bfloat16)
    out_ref[...] = jnp.dot(
        weight_ref[...], jnp.concatenate([rows, rows], axis=0), preferred_element_type=jnp.float32
    ).astype(jnp.bfloat16)


def vmem(count):
    return [pl.BlockSpec(memory_space=pltpu.VMEM)] * count


def dispatch(hidden, gain, ids, flight):
    return pl.pallas_call(
        functools.partial(dispatch_kernel, flight),
        out_shape=jax.ShapeDtypeStruct((flight * CAP, hidden.shape[1]), jnp.bfloat16),
        in_specs=vmem(3),
        out_specs=vmem(1)[0],
        name="dispatch",
    )(hidden, gain, ids)


def shares(hidden, gain, ids, router, flight):
    rows, width = hidden.shape
    return pl.pallas_call(
        functools.partial(shares_kernel, flight),
        out_shape=jax.ShapeDtypeStruct((rows, 2 * flight * CAP), jnp.bfloat16),
        in_specs=vmem(4),
        out_specs=vmem(1)[0],
        cost_estimate=pl.CostEstimate(
            flops=2 * rows * width * router.shape[1],
            bytes_accessed=2 * (hidden.size + router.size),
            transcendentals=rows * router.shape[1],
        ),
        name="shares",
    )(hidden, gain, ids, router)


def combine(weight, parts):
    rows = weight.shape[0]
    depth, width = parts[0].shape
    piece = min(width, 1024)
    block = pl.BlockSpec((depth, piece), lambda i: (0, i))
    return pl.pallas_call(
        combine_kernel,
        out_shape=jax.ShapeDtypeStruct((rows, width), jnp.bfloat16),
        grid=(width // piece,),
        in_specs=[pl.BlockSpec(weight.shape, lambda i: (0, 0))] + [block] * len(parts),
        out_specs=pl.BlockSpec((rows, piece), lambda i: (0, i)),
        name="combine",
    )(weight, *parts)


def expert_rows(rows, gate_weight, up_weight, down_weight):
    gate_act = jnp.dot(rows, gate_weight, preferred_element_type=jnp.float32)
    up_act = jnp.dot(rows, up_weight, preferred_element_type=jnp.float32)
    hidden_act = (jax.nn.silu(gate_act) * up_act).astype(jnp.bfloat16)
    return jnp.dot(hidden_act, down_weight, preferred_element_type=jnp.float32).astype(
        jnp.bfloat16
    )


def shards(hidden, norm_gain, router_weight, expert_ids, gate_weight, up_weight, down_weight):
    devices = lax.axis_size("expert")
    flight = devices // SPLIT
    width = hidden.shape[1]
    gain = norm_gain[None, :]
    ids = expert_ids.T
    outgoing = dispatch(hidden, gain, ids, flight)
    sending = jnp.tile(outgoing.reshape(flight, CAP, width), (SPLIT, 1, 1))
    arrived = lax.all_to_all(sending, "expert", split_axis=0, concat_axis=0, tiled=True)
    weight = shares(hidden, gain, ids, router_weight, flight)
    partial = expert_rows(
        arrived.reshape(-1, width), gate_weight[0], up_weight[0], down_weight[0]
    )
    returned = lax.all_to_all(
        partial.reshape(devices, CAP, width), "expert", split_axis=0, concat_axis=0, tiled=True
    )
    returned = returned.reshape(SPLIT, flight * CAP, width)
    return combine(weight, [returned[m] for m in range(SPLIT)])


def solution(mesh):
    tokens = P(("group", "expert"), None)
    sliced = P("expert", None, None)
    return jax.shard_map(
        shards,
        mesh=mesh,
        in_specs=(tokens, P(), P(), tokens, sliced, sliced, sliced),
        out_specs=tokens,
        check_vma=False,
    )
```

```python
import functools

import jax
import jax.numpy as jnp
from jax import lax
from jax.experimental import pallas as pl
from jax.experimental.pallas import tpu as pltpu
from jax.sharding import PartitionSpec as P

SPLIT = 4
CAP = 16
CHUNKS = 2
EPS = 1e-06
VMEM_LIMIT = 16 * 1024 * 1024
PIECE = 512


def slots_of(ids, me, flight):
    tokens = ids.shape[1]
    named = jnp.concatenate(
        [
            jnp.max((ids == (me ^ k)).astype(jnp.float32), axis=0, keepdims=True)
            for k in range(flight)
        ],
        axis=0,
    )
    earlier = lax.broadcasted_iota(jnp.int32, (tokens, tokens), 0) < lax.broadcasted_iota(
        jnp.int32, (tokens, tokens), 1
    )
    place = jnp.dot(
        named.astype(jnp.bfloat16),
        earlier.astype(jnp.float32).astype(jnp.bfloat16),
        preferred_element_type=jnp.float32,
    )
    return named, place


def spread(named, place, value, flight):
    size = CAP // CHUNKS
    slot = lax.broadcasted_iota(jnp.int32, (size, named.shape[1]), 0)
    return jnp.concatenate(
        [
            jnp.where(
                (place[k : k + 1] == (slot + c * size).astype(jnp.float32))
                & (named[k : k + 1] > 0.0),
                value[k : k + 1],
                0.0,
            )
            for c in range(CHUNKS)
            for k in range(flight)
        ],
        axis=0,
    )


def inv_rms_of(hidden_ref):
    rows, width = hidden_ref.shape
    piece = min(width, PIECE)
    total = jnp.zeros((rows, 1), jnp.float32)
    for i in range(width // piece):
        x = hidden_ref[:, i * piece : (i + 1) * piece].astype(jnp.float32)
        total = total + jnp.sum(x * x, axis=1, keepdims=True)
    return lax.rsqrt(total / width + EPS)


def normed_piece(hidden_ref, gain_ref, inv_rms, cols):
    x = hidden_ref[:, cols].astype(jnp.float32)
    return (x * inv_rms * gain_ref[:, cols].astype(jnp.float32)).astype(jnp.bfloat16)


def dispatch_kernel(flight, me_ref, hidden_ref, gain_ref, ids_ref, *out_refs):
    width = hidden_ref.shape[1]
    piece = min(width, PIECE)
    inv_rms = inv_rms_of(hidden_ref)
    named, place = slots_of(ids_ref[...], me_ref[0], flight)
    select = spread(named, place, named, flight).astype(jnp.bfloat16)
    size = CAP // CHUNKS
    for i in range(width // piece):
        cols = pl.ds(i * piece, piece)
        normed = normed_piece(hidden_ref, gain_ref, inv_rms, cols)
        rows = jnp.dot(select, normed, preferred_element_type=jnp.float32)
        for at, out_ref in enumerate(out_refs):
            out_ref[:, cols] = rows[at * size : (at + 1) * size].astype(jnp.bfloat16)


def shares_kernel(flight, me_ref, hidden_ref, gain_ref, ids_ref, router_ref, out_ref):
    width = hidden_ref.shape[1]
    experts = router_ref.shape[1]
    piece = min(width, PIECE)
    inv_rms = inv_rms_of(hidden_ref)
    logits = jnp.zeros((hidden_ref.shape[0], experts), jnp.float32)
    for i in range(width // piece):
        cols = pl.ds(i * piece, piece)
        normed = normed_piece(hidden_ref, gain_ref, inv_rms, cols)
        logits += jnp.dot(normed, router_ref[cols, :], preferred_element_type=jnp.float32)
    logits = logits.T
    raised = jnp.exp(logits - jnp.max(logits, axis=0, keepdims=True))
    probs = raised / jnp.sum(raised, axis=0, keepdims=True)
    ids = ids_ref[...]
    expert = lax.broadcasted_iota(jnp.int32, probs.shape, 0)
    picked = jnp.zeros(probs.shape, jnp.float32)
    for k in range(ids.shape[0]):
        picked = jnp.where(ids[k : k + 1] == expert, probs, picked)
    me = me_ref[0]
    named, place = slots_of(ids, me, flight)
    flying = jnp.concatenate(
        [
            jnp.sum(jnp.where(expert == (me ^ k), probs, 0.0), axis=0, keepdims=True)
            for k in range(flight)
        ],
        axis=0,
    )
    share = flying / jnp.sum(picked, axis=0, keepdims=True)
    weight = spread(named, place, share, flight).T
    high = weight.astype(jnp.bfloat16)
    low = (weight - high.astype(jnp.float32)).astype(jnp.bfloat16)
    out_ref[...] = jnp.concatenate([high, low], axis=1)


def expert_kernel(rows_ref, gate_ref, up_ref, down_ref, out_ref):
    rows = rows_ref[...]
    gate_act = jnp.dot(rows, gate_ref[0], preferred_element_type=jnp.float32)
    up_act = jnp.dot(rows, up_ref[0], preferred_element_type=jnp.float32)
    hidden_act = (jax.nn.silu(gate_act) * up_act).astype(jnp.bfloat16)
    width = out_ref.shape[1]
    piece = min(width, PIECE)
    for i in range(width // piece):
        cols = pl.ds(i * piece, piece)
        out_ref[:, cols] = jnp.dot(
            hidden_act, down_ref[0, :, cols], preferred_element_type=jnp.float32
        ).astype(jnp.bfloat16)


def combine_kernel(weight_ref, *refs):
    *parts, out_ref = refs
    rows = jnp.concatenate([part[...].astype(jnp.float32) for part in parts], axis=0)
    rows = rows.astype(jnp.bfloat16)
    out_ref[...] = jnp.dot(
        weight_ref[...], jnp.concatenate([rows, rows], axis=0), preferred_element_type=jnp.float32
    ).astype(jnp.bfloat16)


def vmem(count):
    return [pl.BlockSpec(memory_space=pltpu.VMEM)] * count


def params():
    return pltpu.CompilerParams(vmem_limit_bytes=VMEM_LIMIT)


def dispatch(me, hidden, gain, ids, flight):
    shape = jax.ShapeDtypeStruct((CAP // CHUNKS, hidden.shape[1]), jnp.bfloat16)
    count = CHUNKS * flight
    out = pl.pallas_call(
        functools.partial(dispatch_kernel, flight),
        out_shape=[shape] * count,
        in_specs=[pl.BlockSpec(memory_space=pltpu.SMEM)] + vmem(3),
        out_specs=vmem(count),
        compiler_params=params(),
        name="dispatch",
    )(me, hidden, gain, ids)
    return [out[c * flight : (c + 1) * flight] for c in range(CHUNKS)]


def shares(me, hidden, gain, ids, router, flight):
    rows, width = hidden.shape
    return pl.pallas_call(
        functools.partial(shares_kernel, flight),
        out_shape=jax.ShapeDtypeStruct((rows, 2 * flight * CAP), jnp.bfloat16),
        in_specs=[pl.BlockSpec(memory_space=pltpu.SMEM)] + vmem(4),
        out_specs=vmem(1)[0],
        compiler_params=params(),
        cost_estimate=pl.CostEstimate(
            flops=2 * rows * width * router.shape[1],
            bytes_accessed=2 * (hidden.size + router.size),
            transcendentals=rows * router.shape[1],
        ),
        name="shares",
    )(me, hidden, gain, ids, router)


def expert(rows, gate_weight, up_weight, down_weight):
    count = gate_weight.size + up_weight.size + down_weight.size
    return pl.pallas_call(
        expert_kernel,
        out_shape=jax.ShapeDtypeStruct(rows.shape, jnp.bfloat16),
        in_specs=vmem(4),
        out_specs=vmem(1)[0],
        compiler_params=params(),
        cost_estimate=pl.CostEstimate(
            flops=2 * rows.shape[0] * count, bytes_accessed=2 * count, transcendentals=0
        ),
        name="expert",
    )(rows, gate_weight, up_weight, down_weight)


def combine(weight, parts):
    rows = weight.shape[0]
    width = parts[0].shape[1]
    piece = min(width, 1024)
    return pl.pallas_call(
        combine_kernel,
        out_shape=jax.ShapeDtypeStruct((rows, width), jnp.bfloat16),
        grid=(width // piece,),
        in_specs=[pl.BlockSpec(weight.shape, lambda i: (0, 0))]
        + [pl.BlockSpec((part.shape[0], piece), lambda i: (0, i)) for part in parts],
        out_specs=pl.BlockSpec((rows, piece), lambda i: (0, i)),
        compiler_params=params(),
        name="combine",
    )(weight, *parts)


def in_plane(blocks, flight):
    got = list(blocks)
    for k in reversed(range(1, flight)):
        pairs = [
            (m * flight + e, m * flight + (e ^ k)) for m in range(SPLIT) for e in range(flight)
        ]
        got[k] = lax.ppermute(blocks[k], "expert", pairs)
    return got


def end_pair(rows, flight, sides=(0, 1, 2, 3)):
    pairs = [(m * flight + e, (m ^ 1) * flight + e) for m in sides for e in range(flight)]
    return lax.ppermute(rows, "expert", pairs)


def middle_pair(rows, flight):
    pairs = [(m * flight + e, (3 - m) * flight + e) for m in (1, 2) for e in range(flight)]
    return lax.ppermute(rows, "expert", pairs)


def plus(*terms):
    total = terms[0].astype(jnp.float32)
    for term in terms[1:]:
        total = total + term.astype(jnp.float32)
    return total.astype(jnp.bfloat16)


def shards(hidden, norm_gain, router_weight, expert_ids, gate_weight, up_weight, down_weight):
    devices = lax.axis_size("expert")
    flight = devices // SPLIT
    gain = norm_gain[None, :]
    ids = expert_ids.T
    index = lax.axis_index("expert")
    member = index // flight
    outer = (member == 0) | (member == SPLIT - 1)
    me = (index % flight).astype(jnp.int32)[None]

    def partial(rows):
        return expert(rows, gate_weight, up_weight, down_weight)

    sent = dispatch(me, hidden, gain, ids, flight)
    own = [jnp.concatenate(in_plane(blocks, flight), axis=0) for blocks in sent]
    near = [end_pair(x, flight) for x in own]
    far_in = [middle_pair(x, flight) for x in own]
    last_in = [middle_pair(x, flight) for x in near]
    near_part = [partial(x) for x in near]
    two = [
        end_pair(jnp.where(outer, n, f), flight) for n, f in zip(near_part, far_in)
    ]
    far_part = [partial(jnp.where(outer, t, f)) for t, f in zip(two, far_in)]
    three = [
        end_pair(jnp.where(outer, f, x), flight) for f, x in zip(far_part, last_in)
    ]
    last_part = [partial(jnp.where(outer, t, x)) for t, x in zip(three, last_in)]
    mid = [middle_pair(plus(f, t), flight) for f, t in zip(far_part, three)]
    four = [end_pair(x, flight, (0, 3)) for x in last_part]
    mid2 = [middle_pair(plus(x, f), flight) for x, f in zip(last_part, four)]
    five = [end_pair(plus(n, x), flight, (1, 2)) for n, x in zip(near_part, mid2)]
    own_part = partial(jnp.concatenate(own, axis=0))
    weight = shares(me, hidden, gain, ids, router_weight, flight)
    back = []
    depth = own[0].shape[0]
    size = depth // flight
    for c in range(CHUNKS):
        mine = own_part[c * depth : (c + 1) * depth]
        done = jnp.where(outer, plus(mine, five[c]), plus(mine, two[c], mid[c]))
        back += in_plane([done[k * size : (k + 1) * size] for k in range(flight)], flight)
    return combine(weight, back)


def solution(mesh):
    tokens = P(("group", "expert"), None)
    sliced = P("expert", None, None)
    return jax.shard_map(
        shards,
        mesh=mesh,
        in_specs=(tokens, P(), P(), tokens, sliced, sliced, sliced),
        out_specs=tokens,
        check_vma=False,
    )
```

```python
import functools

import jax
import jax.numpy as jnp
from jax import lax
from jax.experimental import pallas as pl
from jax.experimental.pallas import tpu as pltpu
from jax.sharding import PartitionSpec as P

SPLIT = 4
CAP = 16
EPS = 1e-06
PIECE = 512
COLUMNS = 512
VMEM_LIMIT = 16 * 1024 * 1024


def slots_of(ids, me, flight):
    tokens = ids.shape[1]
    named = jnp.concatenate(
        [
            jnp.max((ids == (me ^ k)).astype(jnp.float32), axis=0, keepdims=True)
            for k in range(flight)
        ],
        axis=0,
    )
    earlier = lax.broadcasted_iota(jnp.int32, (tokens, tokens), 0) < lax.broadcasted_iota(
        jnp.int32, (tokens, tokens), 1
    )
    place = jnp.dot(
        named.astype(jnp.bfloat16),
        earlier.astype(jnp.float32).astype(jnp.bfloat16),
        preferred_element_type=jnp.float32,
    )
    return named, place


def spread(named, place, value, flight):
    slot = lax.broadcasted_iota(jnp.int32, (CAP, named.shape[1]), 0).astype(jnp.float32)
    return jnp.concatenate(
        [
            jnp.where(
                (place[k : k + 1] == slot) & (named[k : k + 1] > 0.0), value[k : k + 1], 0.0
            )
            for k in range(flight)
        ],
        axis=0,
    )


def inv_rms_of(hidden_ref):
    rows, width = hidden_ref.shape
    piece = min(width, PIECE)
    total = jnp.zeros((rows, 1), jnp.float32)
    for i in range(width // piece):
        x = hidden_ref[:, i * piece : (i + 1) * piece].astype(jnp.float32)
        total = total + jnp.sum(x * x, axis=1, keepdims=True)
    return lax.rsqrt(total / width + EPS)


def normed_piece(hidden_ref, gain_ref, inv_rms, cols):
    x = hidden_ref[:, cols].astype(jnp.float32)
    lanes = gain_ref.shape[1]
    gain = jnp.concatenate(
        [
            gain_ref[row : row + 1].astype(jnp.float32)
            for row in range(cols.start // lanes, (cols.start + cols.size) // lanes)
        ],
        axis=1,
    )
    return (x * inv_rms * gain).astype(jnp.bfloat16)


def fetch(sources, targets, sems):
    copies = [
        pltpu.make_async_copy(source, target, sems.at[at])
        for at, (source, target) in enumerate(zip(sources, targets))
    ]
    for copy in copies:
        copy.start()
    for copy in copies:
        copy.wait()


def dispatch_kernel(flight, me_ref, outer_ref, inner_ref, *refs):
    out_refs = refs[3 : 3 + flight]
    hidden_ref, gain_ref, ids_ref, sems = refs[3 + flight :]
    fetch(refs[:3], (hidden_ref, gain_ref, ids_ref), sems)
    width = hidden_ref.shape[1]
    piece = min(width, PIECE)
    inv_rms = inv_rms_of(hidden_ref)
    named, place = slots_of(ids_ref[...], me_ref[0], flight)
    select = spread(named, place, named, flight).astype(jnp.bfloat16)
    for i in range(width // piece):
        cols = pl.ds(i * piece, piece)
        normed = normed_piece(hidden_ref, gain_ref, inv_rms, cols)
        rows = jnp.dot(select, normed, preferred_element_type=jnp.float32)
        for at, out_ref in enumerate(out_refs):
            out_ref[:, cols] = rows[at * CAP : (at + 1) * CAP].astype(jnp.bfloat16)


def shares_kernel(flight, me_ref, *refs):
    out_ref = refs[-6]
    hidden_ref, gain_ref, ids_ref, router_ref, sems = refs[-5:]
    fetch(refs[:4], (hidden_ref, gain_ref, ids_ref, router_ref), sems)
    width = hidden_ref.shape[1]
    experts = router_ref.shape[1]
    piece = min(width, PIECE)
    inv_rms = inv_rms_of(hidden_ref)
    logits = jnp.zeros((hidden_ref.shape[0], experts), jnp.float32)
    for i in range(width // piece):
        cols = pl.ds(i * piece, piece)
        normed = normed_piece(hidden_ref, gain_ref, inv_rms, cols)
        logits += jnp.dot(normed, router_ref[cols, :], preferred_element_type=jnp.float32)
    logits = logits.T
    raised = jnp.exp(logits - jnp.max(logits, axis=0, keepdims=True))
    probs = raised / jnp.sum(raised, axis=0, keepdims=True)
    ids = ids_ref[...]
    expert = lax.broadcasted_iota(jnp.int32, probs.shape, 0)
    picked = jnp.zeros(probs.shape, jnp.float32)
    for k in range(ids.shape[0]):
        picked = jnp.where(ids[k : k + 1] == expert, probs, picked)
    me = me_ref[0]
    named, place = slots_of(ids, me, flight)
    flying = jnp.concatenate(
        [
            jnp.sum(jnp.where(expert == (me ^ k), probs, 0.0), axis=0, keepdims=True)
            for k in range(flight)
        ],
        axis=0,
    )
    share = flying / jnp.sum(picked, axis=0, keepdims=True)
    weight = spread(named, place, share, flight).T
    high = weight.astype(jnp.bfloat16)
    low = (weight - high.astype(jnp.float32)).astype(jnp.bfloat16)
    out_ref[...] = jnp.concatenate([high, low], axis=1)


def expert_kernel(rows_ref, gate_ref, up_ref, down_ref, *refs):
    out_ref = refs[-1]
    rows = rows_ref[...]
    gate_act = jnp.dot(rows, gate_ref[0], preferred_element_type=jnp.float32)
    up_act = jnp.dot(rows, up_ref[0], preferred_element_type=jnp.float32)
    hidden_act = (jax.nn.silu(gate_act) * up_act).astype(jnp.bfloat16)
    width = out_ref.shape[1]
    piece = min(width, PIECE)
    for i in range(width // piece):
        cols = pl.ds(i * piece, piece)
        out_ref[:, cols] = jnp.dot(
            hidden_act, down_ref[0, :, cols], preferred_element_type=jnp.float32
        ).astype(jnp.bfloat16)


def expert_if_kernel(flag_ref, *refs):
    @pl.when(flag_ref[0] != 0)
    def _():
        expert_kernel(*refs)

    @pl.when(flag_ref[0] == 0)
    def _():
        refs[-1][...] = jnp.zeros_like(refs[-1])


def combine_kernel(weight_ref, *refs):
    *parts, out_ref, block_ref, sems = refs
    width = block_ref.shape[1]
    piece = min(width, COLUMNS)
    weight = weight_ref[...]
    copies = []
    for i in range(width // piece):
        cols = pl.ds(i * piece, piece)
        rows = jnp.concatenate([part[:, cols] for part in parts], axis=0)
        block_ref[:, cols] = jnp.dot(
            weight, jnp.concatenate([rows, rows], axis=0), preferred_element_type=jnp.float32
        ).astype(jnp.bfloat16)
        copy = pltpu.make_async_copy(block_ref.at[:, cols], out_ref.at[:, cols], sems.at[i])
        copy.start()
        copies.append(copy)
    for copy in copies:
        copy.wait()


def touch_kernel(*refs):
    refs[-1][...] = jnp.zeros_like(refs[-1])


def choose_kernel(flag_ref, ours_ref, theirs_ref, *refs):
    out_ref = refs[-1]

    @pl.when(flag_ref[0] != 0)
    def _():
        out_ref[...] = ours_ref[...]

    @pl.when(flag_ref[0] == 0)
    def _():
        out_ref[...] = theirs_ref[...]


def choose(flag, ours, theirs, after=()):
    return pl.pallas_call(
        choose_kernel,
        out_shape=jax.ShapeDtypeStruct(ours.shape, ours.dtype),
        in_specs=smem(1) + vmem(2) + anywhere(len(after)),
        out_specs=vmem(1)[0],
        compiler_params=params(),
        name="choose",
    )(flag, ours, theirs, *after)


def join_kernel(count, *refs):
    out_ref = refs[-1]
    depth = refs[0].shape[0]
    for at in range(count):
        out_ref[at * depth : (at + 1) * depth] = refs[at][...]


def join(parts, after=()):
    rows, width = parts[0].shape
    return pl.pallas_call(
        functools.partial(join_kernel, len(parts)),
        out_shape=jax.ShapeDtypeStruct((rows * len(parts), width), jnp.bfloat16),
        in_specs=vmem(len(parts)) + anywhere(len(after)),
        out_specs=vmem(1)[0],
        compiler_params=params(),
        name="join",
    )(*parts, *after)


def touch_any(*arrays):
    return pl.pallas_call(
        touch_kernel,
        out_shape=jax.ShapeDtypeStruct((8, 128), jnp.float32),
        in_specs=anywhere(len(arrays)),
        out_specs=vmem(1)[0],
        compiler_params=params(),
        name="seen",
    )(*arrays)


def mix_kernel(terms, *refs):
    out_refs = refs[terms[1] :]
    total = refs[0][...].astype(jnp.float32)
    for ref in refs[1 : terms[0]]:
        total = total + ref[...].astype(jnp.float32)
    depth = out_refs[0].shape[0]
    for at, out_ref in enumerate(out_refs):
        out_ref[...] = total[at * depth : (at + 1) * depth].astype(jnp.bfloat16)


def vmem(count):
    return [pl.BlockSpec(memory_space=pltpu.VMEM)] * count


def anywhere(count):
    return [pl.BlockSpec(memory_space=pl.ANY)] * count


def smem(count):
    return [pl.BlockSpec(memory_space=pltpu.SMEM)] * count


def params(limit=VMEM_LIMIT):
    return pltpu.CompilerParams(vmem_limit_bytes=limit)


def dispatch(scalars, hidden, gain, ids, flight):
    shape = jax.ShapeDtypeStruct((CAP, hidden.shape[1]), jnp.bfloat16)
    return pl.pallas_call(
        functools.partial(dispatch_kernel, flight),
        out_shape=[shape] * flight,
        in_specs=smem(len(scalars)) + anywhere(3),
        out_specs=vmem(flight),
        scratch_shapes=[pltpu.VMEM(x.shape, x.dtype) for x in (hidden, gain, ids)]
        + [pltpu.SemaphoreType.DMA((3,))],
        compiler_params=params(),
        cost_estimate=pl.CostEstimate(flops=1 << 17, bytes_accessed=128, transcendentals=0),
        name="dispatch",
    )(*scalars, hidden, gain, ids)


def shares(me, hidden, gain, ids, router, flight, *after):
    rows, width = hidden.shape
    return pl.pallas_call(
        functools.partial(shares_kernel, flight),
        out_shape=jax.ShapeDtypeStruct((rows, 2 * flight * CAP), jnp.bfloat16),
        in_specs=smem(1) + anywhere(4 + len(after)),
        out_specs=vmem(1)[0],
        scratch_shapes=[pltpu.VMEM(x.shape, x.dtype) for x in (hidden, gain, ids, router)]
        + [pltpu.SemaphoreType.DMA((4,))],
        compiler_params=params(),
        name="shares",
    )(me, hidden, gain, ids, router, *after)


def touch(array, *after):
    return pl.pallas_call(
        touch_kernel,
        out_shape=jax.ShapeDtypeStruct((8, 128), jnp.float32),
        in_specs=vmem(1) + anywhere(len(after)),
        out_specs=vmem(1)[0],
        compiler_params=params(),
        name="touch",
    )(array, *after)


def mix(terms, pieces=1, after=()):
    rows, width = terms[0].shape
    shape = jax.ShapeDtypeStruct((rows // pieces, width), jnp.bfloat16)
    return pl.pallas_call(
        functools.partial(mix_kernel, (len(terms), len(terms) + len(after))),
        out_shape=[shape] * pieces,
        in_specs=vmem(len(terms)) + anywhere(len(after)),
        out_specs=vmem(pieces),
        compiler_params=params(),
        name="mix",
    )(*terms, *after)


def finish_kernel(count, flag_ref, own_ref, *refs):
    ours, theirs = refs[: count[0]], refs[count[0] : count[1]]
    out_refs = refs[count[1] + count[2] :]
    depth = out_refs[0].shape[0]

    def add(others):
        total = own_ref[...].astype(jnp.float32)
        for ref in others:
            total = total + ref[...].astype(jnp.float32)
        for at, out_ref in enumerate(out_refs):
            out_ref[...] = total[at * depth : (at + 1) * depth].astype(jnp.bfloat16)

    @pl.when(flag_ref[0] != 0)
    def _():
        add(ours)

    @pl.when(flag_ref[0] == 0)
    def _():
        add(theirs)


def finish(flag, own, ours, theirs, pieces, after=()):
    rows, width = own.shape
    shape = jax.ShapeDtypeStruct((rows // pieces, width), jnp.bfloat16)
    return pl.pallas_call(
        functools.partial(
            finish_kernel, (len(ours), len(ours) + len(theirs), len(after))
        ),
        out_shape=[shape] * pieces,
        in_specs=smem(1) + vmem(1 + len(ours) + len(theirs)) + anywhere(len(after)),
        out_specs=vmem(pieces),
        compiler_params=params(),
        name="finish",
    )(flag, own, *ours, *theirs, *after)


def expert(name, flag, rows, gate_weight, up_weight, down_weight, after=()):
    count = gate_weight.size + up_weight.size + down_weight.size
    flags = [] if flag is None else [flag]
    return pl.pallas_call(
        expert_kernel if flag is None else expert_if_kernel,
        out_shape=jax.ShapeDtypeStruct(rows.shape, jnp.bfloat16),
        in_specs=smem(len(flags)) + vmem(4) + anywhere(len(after)),
        out_specs=vmem(1)[0],
        compiler_params=params(),
        cost_estimate=pl.CostEstimate(
            flops=2 * rows.shape[0] * count, bytes_accessed=2 * count, transcendentals=0
        ),
        name=name,
    )(*flags, rows, gate_weight, up_weight, down_weight, *after)


def combine(weight, parts):
    rows = weight.shape[0]
    width = parts[0].shape[1]
    return pl.pallas_call(
        combine_kernel,
        out_shape=jax.ShapeDtypeStruct((rows, width), jnp.bfloat16),
        in_specs=vmem(1 + len(parts)),
        out_specs=anywhere(1)[0],
        scratch_shapes=[
            pltpu.VMEM((rows, width), jnp.bfloat16),
            pltpu.SemaphoreType.DMA((width // min(width, COLUMNS),)),
        ],
        compiler_params=params(),
        name="combine",
    )(weight, *parts)


def in_plane(rows, k, flight):
    if k == 0:
        return rows
    pairs = [(m * flight + e, m * flight + (e ^ k)) for m in range(SPLIT) for e in range(flight)]
    with jax.named_scope("plane%d" % k):
        return lax.ppermute(rows, "expert", pairs)


def end_pair(rows, flight):
    pairs = [(m * flight + e, (m ^ 1) * flight + e) for m in range(SPLIT) for e in range(flight)]
    return lax.ppermute(rows, "expert", pairs)


def mirror_pair(rows, flight, members):
    pairs = [
        (m * flight + e, (SPLIT - 1 - m) * flight + e if m in members else m * flight + (e ^ 1))
        for m in range(SPLIT)
        for e in range(flight)
    ]
    return lax.ppermute(rows, "expert", pairs)


def shards(hidden, norm_gain, router_weight, expert_ids, gate_weight, up_weight, down_weight):
    devices = lax.axis_size("expert")
    flight = devices // SPLIT
    gain = norm_gain.reshape(-1, 128)
    ids = expert_ids.T
    index = lax.axis_index("expert")
    member = lax.div(index, flight)
    me = lax.rem(index, flight).reshape(1)
    inner_number = lax.rem(lax.div(member + 1, 2), 2)
    at_inner, at_outer = inner_number.reshape(1), (1 - inner_number).reshape(1)
    half = flight // 2
    tick = []

    def then(value):
        tick[:] = [value[0] if isinstance(value, (list, tuple)) else value]
        return value

    def partial(rows, flag=None):
        return then(
            expert("expert", flag, rows, gate_weight, up_weight, down_weight, tuple(tick))
        )

    def pick(ours, theirs):
        return then(choose(at_outer, ours, theirs, tuple(tick)))

    def total(*terms):
        return then(mix(terms, 1, tuple(tick)))[0]

    def seen(*arrays):
        return then(touch_any(*arrays, *tick))

    def end(name, rows):
        with jax.named_scope(name):
            return end_pair(rows, flight)

    def middle(name, rows, members=(1, 2)):
        with jax.named_scope(name):
            return mirror_pair(rows, flight, members)

    hidden, gain, ids = (
        pltpu.with_memory_space_constraint(x, pltpu.HBM) for x in (hidden, gain, ids)
    )
    sent = then(dispatch((me, at_outer, at_inner), hidden, gain, ids, flight))
    came = [in_plane(rows, k, flight) for k, rows in enumerate(sent)]
    own_a = then(join(came[:half], tuple(tick)))
    near_a, far_in_a = end("near_a", own_a), middle("far_in_a", own_a)
    for array in (gate_weight, up_weight, down_weight):
        then(touch(array, *tick))
    own_b = then(join(came[half:], tuple(tick)))
    near_b, far_in_b = end("near_b", own_b), middle("far_in_b", own_b)
    near_part_a = partial(near_a)
    last_in_a = middle("last_in_a", near_a)
    two_a = end("two_a", pick(near_part_a, far_in_a))
    near_part_b = partial(near_b)
    two_b = end("two_b", pick(near_part_b, far_in_b))
    last_in_b = middle("last_in_b", near_b)
    seen(last_in_a)
    far_part_a = partial(pick(two_a, far_in_a))
    three_a = end("three_a", pick(far_part_a, last_in_a))
    across_b = middle("across_b", partial(last_in_b, at_inner))
    far_part_b = partial(pick(two_b, far_in_b))
    three_b = end("three_b", pick(far_part_b, last_in_b))
    mid_a = middle("mid_a", total(far_part_a, three_a))
    last_part_a = partial(pick(three_a, last_in_a))
    four = end("four", pick(last_part_a, total(near_part_b, across_b)))
    mid_b = middle("mid_b", total(far_part_b, three_b))
    direct_b = middle("direct_b", partial(three_b, at_outer), (0, 3))
    seen(mid_a)
    mid2_a = middle("mid2_a", total(last_part_a, four))
    weight = then(shares(me, hidden, gain, ids, router_weight, flight, *tick))
    own_part_b, own_part_a = partial(own_b), partial(own_a)
    seen(mid_b)
    five_a = end("five_a", total(near_part_a, mid2_a))
    done_b = then(
        finish(at_outer, own_part_b, [four, direct_b], [two_b, mid_b], flight - half, tuple(tick))
    )
    done_a = then(finish(at_outer, own_part_a, [five_a], [two_a, mid_a], half, tuple(tick)))
    back = [in_plane(rows, k, flight) for k, rows in enumerate(list(done_a) + list(done_b))]
    return combine(weight, back)


def solution(mesh):
    tokens = P(("group", "expert"), None)
    sliced = P("expert", None, None)
    return jax.shard_map(
        shards,
        mesh=mesh,
        in_specs=(tokens, P(), P(), tokens, sliced, sliced, sliced),
        out_specs=tokens,
        check_vma=False,
    )
```

```python
import functools

import jax
import jax.numpy as jnp
from jax import lax
from jax.experimental import pallas as pl
from jax.experimental.pallas import tpu as pltpu
from jax.sharding import PartitionSpec as P

SPLIT = 4
CAP = 16
EPS = 1e-06
PIECE = 512
COLUMNS = 512
VMEM_LIMIT = 16 * 1024 * 1024


def slots_of(ids, me, flight):
    tokens = ids.shape[1]
    named = jnp.concatenate(
        [
            jnp.max((ids == (me ^ k)).astype(jnp.float32), axis=0, keepdims=True)
            for k in range(flight)
        ],
        axis=0,
    )
    earlier = lax.broadcasted_iota(jnp.int32, (tokens, tokens), 0) < lax.broadcasted_iota(
        jnp.int32, (tokens, tokens), 1
    )
    place = jnp.dot(
        named.astype(jnp.bfloat16),
        earlier.astype(jnp.float32).astype(jnp.bfloat16),
        preferred_element_type=jnp.float32,
    )
    return named, place


def spread(named, place, value, flight):
    slot = lax.broadcasted_iota(jnp.int32, (CAP, named.shape[1]), 0).astype(jnp.float32)
    return jnp.concatenate(
        [
            jnp.where(
                (place[k : k + 1] == slot) & (named[k : k + 1] > 0.0), value[k : k + 1], 0.0
            )
            for k in range(flight)
        ],
        axis=0,
    )


def inv_rms_of(hidden_ref):
    rows, width = hidden_ref.shape
    piece = min(width, PIECE)
    total = jnp.zeros((rows, 1), jnp.float32)
    for i in range(width // piece):
        x = hidden_ref[:, i * piece : (i + 1) * piece].astype(jnp.float32)
        total = total + jnp.sum(x * x, axis=1, keepdims=True)
    return lax.rsqrt(total / width + EPS)


def normed_piece(hidden_ref, gain_ref, inv_rms, cols):
    x = hidden_ref[:, cols].astype(jnp.float32)
    lanes = gain_ref.shape[1]
    gain = jnp.concatenate(
        [
            gain_ref[row : row + 1].astype(jnp.float32)
            for row in range(cols.start // lanes, (cols.start + cols.size) // lanes)
        ],
        axis=1,
    )
    return (x * inv_rms * gain).astype(jnp.bfloat16)


def fetch(sources, targets, sems):
    copies = [
        pltpu.make_async_copy(source, target, sems.at[at])
        for at, (source, target) in enumerate(zip(sources, targets))
    ]
    for copy in copies:
        copy.start()
    for copy in copies:
        copy.wait()


def dispatch_kernel(flight, me_ref, outer_ref, inner_ref, *refs):
    out_refs = refs[3:-4]
    hidden_ref, gain_ref, ids_ref, sems = refs[-4:]
    fetch(refs[:3], (hidden_ref, gain_ref, ids_ref), sems)
    width = hidden_ref.shape[1]
    piece = min(width, PIECE)
    inv_rms = inv_rms_of(hidden_ref)
    named, place = slots_of(ids_ref[...], me_ref[0], flight)
    select = spread(named, place, named, flight).astype(jnp.bfloat16)
    for i in range(width // piece):
        cols = pl.ds(i * piece, piece)
        normed = normed_piece(hidden_ref, gain_ref, inv_rms, cols)
        rows = jnp.dot(select, normed, preferred_element_type=jnp.float32)
        for at, out_ref in enumerate(out_refs):
            out_ref[:, cols] = rows[at * CAP : (at + 1) * CAP].astype(jnp.bfloat16)


def shares_kernel(flight, me_ref, *refs):
    out_ref = refs[-6]
    hidden_ref, gain_ref, ids_ref, router_ref, sems = refs[-5:]
    fetch(refs[:4], (hidden_ref, gain_ref, ids_ref, router_ref), sems)
    width = hidden_ref.shape[1]
    experts = router_ref.shape[1]
    piece = min(width, PIECE)
    inv_rms = inv_rms_of(hidden_ref)
    logits = jnp.zeros((hidden_ref.shape[0], experts), jnp.float32)
    for i in range(width // piece):
        cols = pl.ds(i * piece, piece)
        normed = normed_piece(hidden_ref, gain_ref, inv_rms, cols)
        logits += jnp.dot(normed, router_ref[cols, :], preferred_element_type=jnp.float32)
    logits = logits.T
    raised = jnp.exp(logits - jnp.max(logits, axis=0, keepdims=True))
    probs = raised / jnp.sum(raised, axis=0, keepdims=True)
    ids = ids_ref[...]
    expert = lax.broadcasted_iota(jnp.int32, probs.shape, 0)
    picked = jnp.zeros(probs.shape, jnp.float32)
    for k in range(ids.shape[0]):
        picked = jnp.where(ids[k : k + 1] == expert, probs, picked)
    me = me_ref[0]
    named, place = slots_of(ids, me, flight)
    flying = jnp.concatenate(
        [
            jnp.sum(jnp.where(expert == (me ^ k), probs, 0.0), axis=0, keepdims=True)
            for k in range(flight)
        ],
        axis=0,
    )
    share = flying / jnp.sum(picked, axis=0, keepdims=True)
    weight = spread(named, place, share, flight).T
    high = weight.astype(jnp.bfloat16)
    low = (weight - high.astype(jnp.float32)).astype(jnp.bfloat16)
    out_ref[...] = jnp.concatenate([high, low], axis=1)


def expert_kernel(rows_ref, gate_ref, up_ref, down_ref, *refs):
    out_ref = refs[-1]
    rows = rows_ref[...]
    gate_act = jnp.dot(rows, gate_ref[0], preferred_element_type=jnp.float32)
    up_act = jnp.dot(rows, up_ref[0], preferred_element_type=jnp.float32)
    hidden_act = (jax.nn.silu(gate_act) * up_act).astype(jnp.bfloat16)
    width = out_ref.shape[1]
    piece = min(width, PIECE)
    for i in range(width // piece):
        cols = pl.ds(i * piece, piece)
        out_ref[:, cols] = jnp.dot(
            hidden_act, down_ref[0, :, cols], preferred_element_type=jnp.float32
        ).astype(jnp.bfloat16)


def expert_if_kernel(flag_ref, *refs):
    @pl.when(flag_ref[0] != 0)
    def _():
        expert_kernel(*refs)

    @pl.when(flag_ref[0] == 0)
    def _():
        refs[-1][...] = jnp.zeros_like(refs[-1])


def combine_kernel(weight_ref, *refs):
    *parts, out_ref, block_ref, sems = refs
    width = block_ref.shape[1]
    piece = min(width, COLUMNS)
    weight = weight_ref[...]
    copies = []
    for i in range(width // piece):
        cols = pl.ds(i * piece, piece)
        rows = jnp.concatenate([part[:, cols] for part in parts], axis=0)
        block_ref[:, cols] = jnp.dot(
            weight, jnp.concatenate([rows, rows], axis=0), preferred_element_type=jnp.float32
        ).astype(jnp.bfloat16)
        copy = pltpu.make_async_copy(block_ref.at[:, cols], out_ref.at[:, cols], sems.at[i])
        copy.start()
        copies.append(copy)
    for copy in copies:
        copy.wait()


def touch_kernel(*refs):
    refs[-1][...] = jnp.zeros_like(refs[-1])


def choose_kernel(flag_ref, ours_ref, theirs_ref, *refs):
    out_ref = refs[-1]

    @pl.when(flag_ref[0] != 0)
    def _():
        out_ref[...] = ours_ref[...]

    @pl.when(flag_ref[0] == 0)
    def _():
        out_ref[...] = theirs_ref[...]


def choose(flag, ours, theirs, after=()):
    return pl.pallas_call(
        choose_kernel,
        out_shape=jax.ShapeDtypeStruct(ours.shape, ours.dtype),
        in_specs=smem(1) + vmem(2) + anywhere(len(after)),
        out_specs=vmem(1)[0],
        compiler_params=params(),
        name="choose",
    )(flag, ours, theirs, *after)


def join_kernel(count, *refs):
    out_ref = refs[-1]
    depth = refs[0].shape[0]
    for at in range(count):
        out_ref[at * depth : (at + 1) * depth] = refs[at][...]


def join(parts, after=()):
    rows, width = parts[0].shape
    return pl.pallas_call(
        functools.partial(join_kernel, len(parts)),
        out_shape=jax.ShapeDtypeStruct((rows * len(parts), width), jnp.bfloat16),
        in_specs=vmem(len(parts)) + anywhere(len(after)),
        out_specs=vmem(1)[0],
        compiler_params=params(),
        name="join",
    )(*parts, *after)


def touch_any(*arrays):
    return pl.pallas_call(
        touch_kernel,
        out_shape=jax.ShapeDtypeStruct((8, 128), jnp.float32),
        in_specs=anywhere(len(arrays)),
        out_specs=vmem(1)[0],
        compiler_params=params(),
        name="seen",
    )(*arrays)


def mix_kernel(terms, *refs):
    out_refs = refs[terms[1] :]
    total = refs[0][...].astype(jnp.float32)
    for ref in refs[1 : terms[0]]:
        total = total + ref[...].astype(jnp.float32)
    depth = out_refs[0].shape[0]
    for at, out_ref in enumerate(out_refs):
        out_ref[...] = total[at * depth : (at + 1) * depth].astype(jnp.bfloat16)


def vmem(count):
    return [pl.BlockSpec(memory_space=pltpu.VMEM)] * count


def anywhere(count):
    return [pl.BlockSpec(memory_space=pl.ANY)] * count


def smem(count):
    return [pl.BlockSpec(memory_space=pltpu.SMEM)] * count


def params(limit=VMEM_LIMIT):
    return pltpu.CompilerParams(vmem_limit_bytes=limit)


def cost(flops, moved):
    return pl.CostEstimate(flops=flops, bytes_accessed=moved, transcendentals=0)


def dispatch(scalars, hidden, gain, ids, flight):
    return pl.pallas_call(
        functools.partial(dispatch_kernel, flight),
        out_shape=[jax.ShapeDtypeStruct((CAP, hidden.shape[1]), jnp.bfloat16)] * flight,
        in_specs=smem(len(scalars)) + anywhere(3),
        out_specs=vmem(flight),
        scratch_shapes=[pltpu.VMEM(x.shape, x.dtype) for x in (hidden, gain, ids)]
        + [pltpu.SemaphoreType.DMA((3,))],
        compiler_params=params(),
        cost_estimate=cost(hidden.size // 4, 128),
        name="dispatch",
    )(*scalars, hidden, gain, ids)


def shares(me, hidden, gain, ids, router, flight, *after):
    rows, width = hidden.shape
    return pl.pallas_call(
        functools.partial(shares_kernel, flight),
        out_shape=jax.ShapeDtypeStruct((rows, 2 * flight * CAP), jnp.bfloat16),
        in_specs=smem(1) + anywhere(4 + len(after)),
        out_specs=vmem(1)[0],
        scratch_shapes=[pltpu.VMEM(x.shape, x.dtype) for x in (hidden, gain, ids, router)]
        + [pltpu.SemaphoreType.DMA((4,))],
        compiler_params=params(),
        cost_estimate=cost(
            2 * hidden.size * router.shape[1], 2 * (hidden.size + router.size)
        ),
        name="shares",
    )(me, hidden, gain, ids, router, *after)


def touch(array, *after):
    return pl.pallas_call(
        touch_kernel,
        out_shape=jax.ShapeDtypeStruct((8, 128), jnp.float32),
        in_specs=vmem(1) + anywhere(len(after)),
        out_specs=vmem(1)[0],
        compiler_params=params(),
        name="touch",
    )(array, *after)


def mix(terms, pieces=1, after=()):
    rows, width = terms[0].shape
    shape = jax.ShapeDtypeStruct((rows // pieces, width), jnp.bfloat16)
    return pl.pallas_call(
        functools.partial(mix_kernel, (len(terms), len(terms) + len(after))),
        out_shape=[shape] * pieces,
        in_specs=vmem(len(terms)) + anywhere(len(after)),
        out_specs=vmem(pieces),
        compiler_params=params(),
        name="mix",
    )(*terms, *after)


def finish_kernel(count, flag_ref, own_ref, *refs):
    ours, theirs = refs[: count[0]], refs[count[0] : count[1]]
    out_refs = refs[count[2] :]
    depth = out_refs[0].shape[0]

    def add(others):
        total = own_ref[...].astype(jnp.float32)
        for ref in others:
            total = total + ref[...].astype(jnp.float32)
        for at, out_ref in enumerate(out_refs):
            out_ref[...] = total[at * depth : (at + 1) * depth].astype(jnp.bfloat16)

    @pl.when(flag_ref[0] != 0)
    def _():
        add(ours)

    @pl.when(flag_ref[0] == 0)
    def _():
        add(theirs)


def finish(flag, own, ours, theirs, pieces, after=()):
    rows, width = own.shape
    count = [len(ours), len(ours) + len(theirs), len(ours) + len(theirs) + len(after)]
    return pl.pallas_call(
        functools.partial(finish_kernel, count),
        out_shape=[jax.ShapeDtypeStruct((rows // pieces, width), jnp.bfloat16)] * pieces,
        in_specs=smem(1) + vmem(1 + count[1]) + anywhere(len(after)),
        out_specs=vmem(pieces),
        compiler_params=params(),
        name="finish",
    )(flag, own, *ours, *theirs, *after)


def expert(flag, rows, gate_weight, up_weight, down_weight, after=()):
    count = gate_weight.size + up_weight.size + down_weight.size
    flags = [] if flag is None else [flag]
    return pl.pallas_call(
        expert_kernel if flag is None else expert_if_kernel,
        out_shape=jax.ShapeDtypeStruct(rows.shape, jnp.bfloat16),
        in_specs=smem(len(flags)) + vmem(4) + anywhere(len(after)),
        out_specs=vmem(1)[0],
        compiler_params=params(),
        cost_estimate=cost(2 * rows.shape[0] * count, 2 * count),
        name="expert",
    )(*flags, rows, gate_weight, up_weight, down_weight, *after)


def combine(weight, parts):
    rows = weight.shape[0]
    width = parts[0].shape[1]
    return pl.pallas_call(
        combine_kernel,
        out_shape=jax.ShapeDtypeStruct((rows, width), jnp.bfloat16),
        in_specs=vmem(1 + len(parts)),
        out_specs=anywhere(1)[0],
        scratch_shapes=[
            pltpu.VMEM((rows, width), jnp.bfloat16),
            pltpu.SemaphoreType.DMA((width // min(width, COLUMNS),)),
        ],
        compiler_params=params(),
        name="combine",
    )(weight, *parts)


def in_plane(rows, k, flight):
    if k == 0:
        return rows
    pairs = [(m * flight + e, m * flight + (e ^ k)) for m in range(SPLIT) for e in range(flight)]
    with jax.named_scope("plane%d" % k):
        return lax.ppermute(rows, "expert", pairs)


def end_pair(rows, flight):
    pairs = [(m * flight + e, (m ^ 1) * flight + e) for m in range(SPLIT) for e in range(flight)]
    return lax.ppermute(rows, "expert", pairs)


def mirror_pair(rows, flight, members):
    pairs = [
        (m * flight + e, (SPLIT - 1 - m) * flight + e if m in members else m * flight + (e ^ 1))
        for m in range(SPLIT)
        for e in range(flight)
    ]
    return lax.ppermute(rows, "expert", pairs)


def inward_shift(rows, flight, near):
    to = {1: 0, 2: 3, 0: 1, 3: 2} if near else {1: 3, 2: 0}
    pairs = [(m * flight + e, to[m] * flight + e) for m in to for e in range(flight)]
    return lax.ppermute(rows, "expert", pairs)


def shards(hidden, norm_gain, router_weight, expert_ids, gate_weight, up_weight, down_weight):
    devices = lax.axis_size("expert")
    flight = devices // SPLIT
    gain = norm_gain.reshape(-1, 128)
    ids = expert_ids.T
    index = lax.axis_index("expert")
    member = lax.div(index, flight)
    me = lax.rem(index, flight).reshape(1)
    inner_number = lax.rem(lax.div(member + 1, 2), 2)
    at_inner, at_outer = inner_number.reshape(1), (1 - inner_number).reshape(1)
    half = flight // 2
    tick = []

    def then(value):
        tick[:] = [value[0] if isinstance(value, (list, tuple)) else value]
        return value

    def partial(rows, flag=None):
        return then(expert(flag, rows, gate_weight, up_weight, down_weight, tuple(tick)))

    def pick(ours, theirs):
        return then(choose(at_outer, ours, theirs, tuple(tick)))

    def total(*terms):
        return then(mix(terms, 1, tuple(tick)))[0]

    def seen(*arrays):
        return then(touch_any(*arrays, *tick))

    def end(name, rows):
        with jax.named_scope(name):
            return end_pair(rows, flight)

    def middle(name, rows, members=(1, 2)):
        with jax.named_scope(name):
            return mirror_pair(rows, flight, members)

    def inward(name, rows, near):
        with jax.named_scope(name):
            return inward_shift(rows, flight, near)

    hidden, gain, ids = (
        pltpu.with_memory_space_constraint(x, pltpu.HBM) for x in (hidden, gain, ids)
    )
    sent = then(dispatch((me, at_outer, at_inner), hidden, gain, ids, flight))
    came = [in_plane(rows, k, flight) for k, rows in enumerate(sent)]
    own_a = then(join(came[:half], tuple(tick)))
    near_a, far_in_a = end("near_a", own_a), middle("far_in_a", own_a)
    for array in (gate_weight, up_weight, down_weight):
        then(touch(array, *tick))
    own_b = then(join(came[half:], tuple(tick)))
    near_b, far_in_b = end("near_b", own_b), middle("far_in_b", own_b)
    near_part_a = partial(near_a)
    last_in_a = middle("last_in_a", near_a)
    two_a = end("two_a", pick(near_part_a, far_in_a))
    near_part_b = partial(near_b)
    two_b = end("two_b", pick(near_part_b, far_in_b))
    last_in_b = middle("last_in_b", near_b)
    seen(last_in_a)
    far_part_a = partial(pick(two_a, far_in_a))
    three_a = end("three_a", pick(far_part_a, last_in_a))
    across_b = middle("across_b", partial(last_in_b, at_inner))
    far_part_b = partial(pick(two_b, far_in_b))
    three_b = end("three_b", pick(far_part_b, last_in_b))
    mid_a = middle("mid_a", total(far_part_a, three_a))
    last_part_a = partial(pick(three_a, last_in_a))
    seen(across_b)
    four = end("four", pick(last_part_a, near_part_a))
    mid_b = middle("mid_b", total(far_part_b, three_b))
    direct_b = middle("direct_b", partial(three_b, at_outer), (0, 3))
    sum_b = inward("sum_b", total(near_part_b, across_b), True)
    seen(mid_a)
    across_a = inward("across_a", total(last_part_a, four), False)
    weight = then(shares(me, hidden, gain, ids, router_weight, flight, *tick))
    own_part_b, own_part_a = partial(own_b), partial(own_a)
    done_b = then(finish(at_outer, own_part_b, [sum_b, direct_b], [two_b, mid_b], half, tuple(tick)))
    done_a = then(finish(at_outer, own_part_a, [four, across_a], [two_a, mid_a], half, tuple(tick)))
    done = list(done_a) + list(done_b)
    back = [in_plane(rows, k, flight) for k, rows in enumerate(done)]
    return combine(weight, back)


def solution(mesh):
    tokens = P(("group", "expert"), None)
    sliced = P("expert", None, None)
    return jax.shard_map(
        shards,
        mesh=mesh,
        in_specs=(tokens, P(), P(), tokens, sliced, sliced, sliced),
        out_specs=tokens,
        check_vma=False,
    )
```

```python
import functools

import jax
import jax.numpy as jnp
from jax import lax
from jax.experimental import pallas as pl
from jax.experimental.pallas import tpu as pltpu
from jax.sharding import PartitionSpec as P

SPLIT = 4
CAP = 16
EPS = 1e-06
PIECE = 512
COLUMNS = 512
VMEM_LIMIT = 16 * 1024 * 1024


def slots_of(ids, me, flight):
    tokens = ids.shape[1]
    named = jnp.concatenate(
        [
            jnp.max((ids == (me ^ k)).astype(jnp.float32), axis=0, keepdims=True)
            for k in range(flight)
        ],
        axis=0,
    )
    earlier = lax.broadcasted_iota(jnp.int32, (tokens, tokens), 0) < lax.broadcasted_iota(
        jnp.int32, (tokens, tokens), 1
    )
    place = jnp.dot(
        named.astype(jnp.bfloat16),
        earlier.astype(jnp.float32).astype(jnp.bfloat16),
        preferred_element_type=jnp.float32,
    )
    return named, place


def spread(named, place, value, flight):
    slot = lax.broadcasted_iota(jnp.int32, (CAP, named.shape[1]), 0).astype(jnp.float32)
    return jnp.concatenate(
        [
            jnp.where(
                (place[k : k + 1] == slot) & (named[k : k + 1] > 0.0), value[k : k + 1], 0.0
            )
            for k in range(flight)
        ],
        axis=0,
    )


def inv_rms_of(hidden_ref):
    rows, width = hidden_ref.shape
    piece = min(width, PIECE)
    total = jnp.zeros((rows, 1), jnp.float32)
    for i in range(width // piece):
        x = hidden_ref[:, i * piece : (i + 1) * piece].astype(jnp.float32)
        total = total + jnp.sum(x * x, axis=1, keepdims=True)
    return lax.rsqrt(total / width + EPS)


def normed_piece(hidden_ref, gain_ref, inv_rms, cols):
    x = hidden_ref[:, cols].astype(jnp.float32)
    lanes = gain_ref.shape[1]
    gain = jnp.concatenate(
        [
            gain_ref[row : row + 1].astype(jnp.float32)
            for row in range(cols.start // lanes, (cols.start + cols.size) // lanes)
        ],
        axis=1,
    )
    return (x * inv_rms * gain).astype(jnp.bfloat16)


def fetch(sources, targets, sems):
    copies = [
        pltpu.make_async_copy(source, target, sems.at[at])
        for at, (source, target) in enumerate(zip(sources, targets))
    ]
    for copy in copies:
        copy.start()
    for copy in copies:
        copy.wait()


def dispatch_kernel(flight, me_ref, outer_ref, inner_ref, *refs):
    out_refs = refs[3:-4]
    hidden_ref, gain_ref, ids_ref, sems = refs[-4:]
    fetch(refs[:3], (hidden_ref, gain_ref, ids_ref), sems)
    width = hidden_ref.shape[1]
    piece = min(width, PIECE)
    inv_rms = inv_rms_of(hidden_ref)
    named, place = slots_of(ids_ref[...], me_ref[0], flight)
    select = spread(named, place, named, flight).astype(jnp.bfloat16)
    for i in range(width // piece):
        cols = pl.ds(i * piece, piece)
        normed = normed_piece(hidden_ref, gain_ref, inv_rms, cols)
        rows = jnp.dot(select, normed, preferred_element_type=jnp.float32)
        for at, out_ref in enumerate(out_refs):
            out_ref[:, cols] = rows[at * CAP : (at + 1) * CAP].astype(jnp.bfloat16)


def shares_kernel(flight, me_ref, *refs):
    out_ref = refs[-6]
    hidden_ref, gain_ref, ids_ref, router_ref, sems = refs[-5:]
    fetch(refs[:4], (hidden_ref, gain_ref, ids_ref, router_ref), sems)
    width = hidden_ref.shape[1]
    experts = router_ref.shape[1]
    piece = min(width, PIECE)
    inv_rms = inv_rms_of(hidden_ref)
    logits = jnp.zeros((hidden_ref.shape[0], experts), jnp.float32)
    for i in range(width // piece):
        cols = pl.ds(i * piece, piece)
        normed = normed_piece(hidden_ref, gain_ref, inv_rms, cols)
        logits += jnp.dot(normed, router_ref[cols, :], preferred_element_type=jnp.float32)
    logits = logits.T
    raised = jnp.exp(logits - jnp.max(logits, axis=0, keepdims=True))
    probs = raised / jnp.sum(raised, axis=0, keepdims=True)
    ids = ids_ref[...]
    expert = lax.broadcasted_iota(jnp.int32, probs.shape, 0)
    picked = jnp.zeros(probs.shape, jnp.float32)
    for k in range(ids.shape[0]):
        picked = jnp.where(ids[k : k + 1] == expert, probs, picked)
    me = me_ref[0]
    named, place = slots_of(ids, me, flight)
    flying = jnp.concatenate(
        [
            jnp.sum(jnp.where(expert == (me ^ k), probs, 0.0), axis=0, keepdims=True)
            for k in range(flight)
        ],
        axis=0,
    )
    share = flying / jnp.sum(picked, axis=0, keepdims=True)
    weight = spread(named, place, share, flight).T
    high = weight.astype(jnp.bfloat16)
    low = (weight - high.astype(jnp.float32)).astype(jnp.bfloat16)
    out_ref[...] = jnp.concatenate([high, low], axis=1)


def expert_kernel(rows_ref, gate_ref, up_ref, down_ref, *refs):
    out_ref = refs[-1]
    rows = rows_ref[...]
    gate_act = jnp.dot(rows, gate_ref[0], preferred_element_type=jnp.float32)
    up_act = jnp.dot(rows, up_ref[0], preferred_element_type=jnp.float32)
    hidden_act = (jax.nn.silu(gate_act) * up_act).astype(jnp.bfloat16)
    width = out_ref.shape[1]
    piece = min(width, PIECE)
    for i in range(width // piece):
        cols = pl.ds(i * piece, piece)
        out_ref[:, cols] = jnp.dot(
            hidden_act, down_ref[0, :, cols], preferred_element_type=jnp.float32
        ).astype(jnp.bfloat16)


def expert_if_kernel(flag_ref, *refs):
    @pl.when(flag_ref[0] != 0)
    def _():
        expert_kernel(*refs)

    @pl.when(flag_ref[0] == 0)
    def _():
        refs[-1][...] = jnp.zeros_like(refs[-1])


def combine_kernel(weight_ref, *refs):
    *parts, out_ref, block_ref, sems = refs
    width = block_ref.shape[1]
    piece = min(width, COLUMNS)
    weight = weight_ref[...]
    copies = []
    for i in range(width // piece):
        cols = pl.ds(i * piece, piece)
        rows = jnp.concatenate([part[:, cols] for part in parts], axis=0)
        block_ref[:, cols] = jnp.dot(
            weight, jnp.concatenate([rows, rows], axis=0), preferred_element_type=jnp.float32
        ).astype(jnp.bfloat16)
        copy = pltpu.make_async_copy(block_ref.at[:, cols], out_ref.at[:, cols], sems.at[i])
        copy.start()
        copies.append(copy)
    for copy in copies:
        copy.wait()


def touch_kernel(*refs):
    refs[-1][...] = jnp.zeros_like(refs[-1])


def choose_kernel(flag_ref, ours_ref, theirs_ref, *refs):
    out_ref = refs[-1]

    @pl.when(flag_ref[0] != 0)
    def _():
        out_ref[...] = ours_ref[...]

    @pl.when(flag_ref[0] == 0)
    def _():
        out_ref[...] = theirs_ref[...]


def choose(flag, ours, theirs, after=()):
    return pl.pallas_call(
        choose_kernel,
        out_shape=jax.ShapeDtypeStruct(ours.shape, ours.dtype),
        in_specs=smem(1) + vmem(2) + anywhere(len(after)),
        out_specs=vmem(1)[0],
        compiler_params=params(),
        name="choose",
    )(flag, ours, theirs, *after)


def join_kernel(count, *refs):
    out_ref = refs[-1]
    depth = refs[0].shape[0]
    for at in range(count):
        out_ref[at * depth : (at + 1) * depth] = refs[at][...]


def join(parts, after=()):
    rows, width = parts[0].shape
    return pl.pallas_call(
        functools.partial(join_kernel, len(parts)),
        out_shape=jax.ShapeDtypeStruct((rows * len(parts), width), jnp.bfloat16),
        in_specs=vmem(len(parts)) + anywhere(len(after)),
        out_specs=vmem(1)[0],
        compiler_params=params(),
        name="join",
    )(*parts, *after)


def touch_any(*arrays):
    return pl.pallas_call(
        touch_kernel,
        out_shape=jax.ShapeDtypeStruct((8, 128), jnp.float32),
        in_specs=anywhere(len(arrays)),
        out_specs=vmem(1)[0],
        compiler_params=params(),
        name="seen",
    )(*arrays)


def mix_kernel(terms, *refs):
    out_refs = refs[terms[1] :]
    total = refs[0][...].astype(jnp.float32)
    for ref in refs[1 : terms[0]]:
        total = total + ref[...].astype(jnp.float32)
    depth = out_refs[0].shape[0]
    for at, out_ref in enumerate(out_refs):
        out_ref[...] = total[at * depth : (at + 1) * depth].astype(jnp.bfloat16)


def vmem(count):
    return [pl.BlockSpec(memory_space=pltpu.VMEM)] * count


def anywhere(count):
    return [pl.BlockSpec(memory_space=pl.ANY)] * count


def smem(count):
    return [pl.BlockSpec(memory_space=pltpu.SMEM)] * count


def params(limit=VMEM_LIMIT):
    return pltpu.CompilerParams(vmem_limit_bytes=limit)


def cost(flops, moved):
    return pl.CostEstimate(flops=flops, bytes_accessed=moved, transcendentals=0)


def dispatch(scalars, hidden, gain, ids, flight):
    return pl.pallas_call(
        functools.partial(dispatch_kernel, flight),
        out_shape=[jax.ShapeDtypeStruct((CAP, hidden.shape[1]), jnp.bfloat16)] * flight,
        in_specs=smem(len(scalars)) + anywhere(3),
        out_specs=vmem(flight),
        scratch_shapes=[pltpu.VMEM(x.shape, x.dtype) for x in (hidden, gain, ids)]
        + [pltpu.SemaphoreType.DMA((3,))],
        compiler_params=params(),
        cost_estimate=cost(hidden.size // 4, 128),
        name="dispatch",
    )(*scalars, hidden, gain, ids)


def shares(me, hidden, gain, ids, router, flight, *after):
    rows, width = hidden.shape
    return pl.pallas_call(
        functools.partial(shares_kernel, flight),
        out_shape=jax.ShapeDtypeStruct((rows, 2 * flight * CAP), jnp.bfloat16),
        in_specs=smem(1) + anywhere(4 + len(after)),
        out_specs=vmem(1)[0],
        scratch_shapes=[pltpu.VMEM(x.shape, x.dtype) for x in (hidden, gain, ids, router)]
        + [pltpu.SemaphoreType.DMA((4,))],
        compiler_params=params(),
        cost_estimate=cost(
            2 * hidden.size * router.shape[1], 2 * (hidden.size + router.size)
        ),
        name="shares",
    )(me, hidden, gain, ids, router, *after)


def touch(array, *after):
    return pl.pallas_call(
        touch_kernel,
        out_shape=jax.ShapeDtypeStruct((8, 128), jnp.float32),
        in_specs=vmem(1) + anywhere(len(after)),
        out_specs=vmem(1)[0],
        compiler_params=params(),
        name="touch",
    )(array, *after)


def mix(terms, pieces=1, after=()):
    rows, width = terms[0].shape
    shape = jax.ShapeDtypeStruct((rows // pieces, width), jnp.bfloat16)
    return pl.pallas_call(
        functools.partial(mix_kernel, (len(terms), len(terms) + len(after))),
        out_shape=[shape] * pieces,
        in_specs=vmem(len(terms)) + anywhere(len(after)),
        out_specs=vmem(pieces),
        compiler_params=params(),
        name="mix",
    )(*terms, *after)


def finish_kernel(count, flag_ref, own_ref, *refs):
    ours, theirs = refs[: count[0]], refs[count[0] : count[1]]
    out_refs = refs[count[2] :]
    depth = out_refs[0].shape[0]

    def add(others):
        total = own_ref[...].astype(jnp.float32)
        for ref in others:
            total = total + ref[...].astype(jnp.float32)
        for at, out_ref in enumerate(out_refs):
            out_ref[...] = total[at * depth : (at + 1) * depth].astype(jnp.bfloat16)

    @pl.when(flag_ref[0] != 0)
    def _():
        add(ours)

    @pl.when(flag_ref[0] == 0)
    def _():
        add(theirs)


def finish(flag, own, ours, theirs, pieces, after=()):
    rows, width = own.shape
    count = [len(ours), len(ours) + len(theirs), len(ours) + len(theirs) + len(after)]
    return pl.pallas_call(
        functools.partial(finish_kernel, count),
        out_shape=[jax.ShapeDtypeStruct((rows // pieces, width), jnp.bfloat16)] * pieces,
        in_specs=smem(1) + vmem(1 + count[1]) + anywhere(len(after)),
        out_specs=vmem(pieces),
        compiler_params=params(),
        name="finish",
    )(flag, own, *ours, *theirs, *after)


def expert(flag, rows, gate_weight, up_weight, down_weight, after=()):
    count = gate_weight.size + up_weight.size + down_weight.size
    flags = [] if flag is None else [flag]
    return pl.pallas_call(
        expert_kernel if flag is None else expert_if_kernel,
        out_shape=jax.ShapeDtypeStruct(rows.shape, jnp.bfloat16),
        in_specs=smem(len(flags)) + vmem(4) + anywhere(len(after)),
        out_specs=vmem(1)[0],
        compiler_params=params(),
        cost_estimate=cost(2 * rows.shape[0] * count, 2 * count),
        name="expert",
    )(*flags, rows, gate_weight, up_weight, down_weight, *after)


def combine(weight, parts):
    rows = weight.shape[0]
    width = parts[0].shape[1]
    return pl.pallas_call(
        combine_kernel,
        out_shape=jax.ShapeDtypeStruct((rows, width), jnp.bfloat16),
        in_specs=vmem(1 + len(parts)),
        out_specs=anywhere(1)[0],
        scratch_shapes=[
            pltpu.VMEM((rows, width), jnp.bfloat16),
            pltpu.SemaphoreType.DMA((width // min(width, COLUMNS),)),
        ],
        compiler_params=params(),
        name="combine",
    )(weight, *parts)


def in_plane(rows, k, flight):
    if k == 0:
        return rows
    pairs = [(m * flight + e, m * flight + (e ^ k)) for m in range(SPLIT) for e in range(flight)]
    with jax.named_scope("plane%d" % k):
        return lax.ppermute(rows, "expert", pairs)


def end_pair(rows, flight):
    pairs = [(m * flight + e, (m ^ 1) * flight + e) for m in range(SPLIT) for e in range(flight)]
    return lax.ppermute(rows, "expert", pairs)


def mirror_pair(rows, flight, members):
    pairs = [
        (m * flight + e, (SPLIT - 1 - m) * flight + e if m in members else m * flight + (e ^ 1))
        for m in range(SPLIT)
        for e in range(flight)
    ]
    return lax.ppermute(rows, "expert", pairs)


def inward_shift(rows, flight, near):
    to = {1: 0, 2: 3} if near else {1: 3, 2: 0}
    pairs = [(m * flight + e, to[m] * flight + e) for m in to for e in range(flight)]
    return lax.ppermute(rows, "expert", pairs)


def shards(hidden, norm_gain, router_weight, expert_ids, gate_weight, up_weight, down_weight):
    devices = lax.axis_size("expert")
    flight = devices // SPLIT
    gain = norm_gain.reshape(-1, 128)
    ids = expert_ids.T
    index = lax.axis_index("expert")
    member = lax.div(index, flight)
    me = lax.rem(index, flight).reshape(1)
    inner_number = lax.rem(lax.div(member + 1, 2), 2)
    at_inner, at_outer = inner_number.reshape(1), (1 - inner_number).reshape(1)
    half = flight // 2
    tick = []

    def then(value):
        tick[:] = [value[0] if isinstance(value, (list, tuple)) else value]
        return value

    def partial(rows, flag=None):
        return then(expert(flag, rows, gate_weight, up_weight, down_weight, tuple(tick)))

    def pick(ours, theirs):
        return then(choose(at_outer, ours, theirs, tuple(tick)))

    def total(*terms):
        return then(mix(terms, 1, tuple(tick)))[0]

    def seen(*arrays):
        return then(touch_any(*arrays, *tick))

    def end(name, rows):
        with jax.named_scope(name):
            return end_pair(rows, flight)

    def middle(name, rows, members=(1, 2)):
        with jax.named_scope(name):
            return mirror_pair(rows, flight, members)

    def inward(name, rows, near):
        with jax.named_scope(name):
            return inward_shift(rows, flight, near)

    hidden, gain, ids = (
        pltpu.with_memory_space_constraint(x, pltpu.HBM) for x in (hidden, gain, ids)
    )
    sent = then(dispatch((me, at_outer, at_inner), hidden, gain, ids, flight))
    came = [in_plane(rows, k, flight) for k, rows in enumerate(sent)]
    own_a = then(join(came[:half], tuple(tick)))
    near_a, far_in_a = end("near_a", own_a), middle("far_in_a", own_a)
    for array in (gate_weight, up_weight, down_weight):
        then(touch(array, *tick))
    own_b = then(join(came[half:], tuple(tick)))
    near_b, far_in_b = end("near_b", own_b), middle("far_in_b", own_b)
    near_part_a = partial(near_a)
    last_in_a = middle("last_in_a", near_a)
    two_a = end("two_a", pick(near_part_a, far_in_a))
    near_part_b = partial(near_b)
    two_b = end("two_b", pick(near_part_b, far_in_b))
    last_in_b = middle("last_in_b", near_b)
    seen(last_in_a)
    far_part_a = partial(pick(two_a, far_in_a))
    three_a = end("three_a", pick(far_part_a, last_in_a))
    across_b = middle("across_b", partial(last_in_b, at_inner))
    far_part_b = partial(pick(two_b, far_in_b))
    three_b = end("three_b", pick(far_part_b, last_in_b))
    mid_a = middle("mid_a", total(far_part_a, three_a))
    last_part_a = partial(pick(three_a, last_in_a))
    seen(across_b)
    four = end("four", pick(last_part_a, near_part_a))
    mid_b = middle("mid_b", total(far_part_b, three_b))
    sum_b = inward("sum_b", total(near_part_b, across_b), True)
    direct_b = middle("direct_b", partial(three_b, at_outer), (0, 3))
    seen(mid_a)
    across_a = inward("across_a", total(last_part_a, four), False)
    weight = then(shares(me, hidden, gain, ids, router_weight, flight, *tick))
    own_part_b, own_part_a = partial(own_b), partial(own_a)
    done_b = then(finish(at_outer, own_part_b, [sum_b, direct_b], [two_b, mid_b], half, tuple(tick)))
    done_a = then(finish(at_outer, own_part_a, [four, across_a], [two_a, mid_a], half, tuple(tick)))
    done = list(done_a) + list(done_b)
    back = [in_plane(rows, k, flight) for k, rows in enumerate(done)]
    return combine(weight, back)


def solution(mesh):
    tokens = P(("group", "expert"), None)
    sliced = P("expert", None, None)
    return jax.shard_map(
        shards,
        mesh=mesh,
        in_specs=(tokens, P(), P(), tokens, sliced, sliced, sliced),
        out_specs=tokens,
        check_vma=False,
    )
```

```python
import functools

import jax
import jax.numpy as jnp
from jax import lax
from jax.experimental import pallas as pl
from jax.experimental.pallas import tpu as pltpu
from jax.sharding import PartitionSpec as P

SPLIT = 4
CAP = 16
EPS = 1e-06
PIECE = 512
COLUMNS = 256
PARTS = 4
VMEM_LIMIT = 16 * 1024 * 1024


def slots_of(ids, me, flight):
    tokens = ids.shape[1]
    named = jnp.concatenate(
        [
            jnp.max((ids == (me ^ k)).astype(jnp.float32), axis=0, keepdims=True)
            for k in range(flight)
        ],
        axis=0,
    )
    earlier = lax.broadcasted_iota(jnp.int32, (tokens, tokens), 0) < lax.broadcasted_iota(
        jnp.int32, (tokens, tokens), 1
    )
    place = jnp.dot(
        named.astype(jnp.bfloat16),
        earlier.astype(jnp.float32).astype(jnp.bfloat16),
        preferred_element_type=jnp.float32,
    )
    return named, place


def spread(named, place, value, flight):
    slot = lax.broadcasted_iota(jnp.int32, (CAP, named.shape[1]), 0).astype(jnp.float32)
    return jnp.concatenate(
        [
            jnp.where(
                (place[k : k + 1] == slot) & (named[k : k + 1] > 0.0), value[k : k + 1], 0.0
            )
            for k in range(flight)
        ],
        axis=0,
    )


def inv_rms_of(hidden_ref):
    rows, width = hidden_ref.shape
    piece = min(width, PIECE)
    total = jnp.zeros((rows, 1), jnp.float32)
    for i in range(width // piece):
        x = hidden_ref[:, i * piece : (i + 1) * piece].astype(jnp.float32)
        total = total + jnp.sum(x * x, axis=1, keepdims=True)
    return lax.rsqrt(total / width + EPS)


def normed_piece(hidden_ref, gain_ref, inv_rms, cols):
    x = hidden_ref[:, cols].astype(jnp.float32)
    lanes = gain_ref.shape[1]
    gain = jnp.concatenate(
        [
            gain_ref[row : row + 1].astype(jnp.float32)
            for row in range(cols.start // lanes, (cols.start + cols.size) // lanes)
        ],
        axis=1,
    )
    return (x * inv_rms * gain).astype(jnp.bfloat16)


def fetch(sources, targets, sems):
    copies = [
        pltpu.make_async_copy(source, target, sems.at[at])
        for at, (source, target) in enumerate(zip(sources, targets))
    ]
    for copy in copies:
        copy.start()
    for copy in copies:
        copy.wait()


def dispatch_kernel(flight, me_ref, outer_ref, inner_ref, *refs):
    out_refs = refs[3:-4]
    hidden_ref, gain_ref, ids_ref, sems = refs[-4:]
    width = hidden_ref.shape[1]
    piece = min(width, PIECE)
    step = width // PARTS
    copies = [
        pltpu.make_async_copy(refs[2], ids_ref, sems.at[0]),
        pltpu.make_async_copy(refs[1], gain_ref, sems.at[1]),
    ]
    for i in range(PARTS):
        cols = pl.ds(i * step, step)
        copies.append(
            pltpu.make_async_copy(refs[0].at[:, cols], hidden_ref.at[:, cols], sems.at[2 + i])
        )
    for copy in copies:
        copy.start()
    copies[0].wait()
    named, place = slots_of(ids_ref[...], me_ref[0], flight)
    select = spread(named, place, named, flight).astype(jnp.bfloat16)
    squares = jnp.zeros((hidden_ref.shape[0], 128), jnp.float32)
    for i in range(PARTS):
        copies[2 + i].wait()
        for first in range(i * step, (i + 1) * step, 128):
            x = hidden_ref[:, first : first + 128].astype(jnp.float32)
            squares = squares + x * x
    inv_rms = lax.rsqrt(jnp.sum(squares, axis=1, keepdims=True) / width + EPS)
    copies[1].wait()
    for i in range(width // piece):
        cols = pl.ds(i * piece, piece)
        normed = normed_piece(hidden_ref, gain_ref, inv_rms, cols)
        rows = jnp.dot(select, normed, preferred_element_type=jnp.float32)
        for at, out_ref in enumerate(out_refs):
            out_ref[:, cols] = rows[at * CAP : (at + 1) * CAP].astype(jnp.bfloat16)


def shares_kernel(flight, me_ref, *refs):
    out_ref = refs[-6]
    hidden_ref, gain_ref, ids_ref, router_ref, sems = refs[-5:]
    fetch(refs[:4], (hidden_ref, gain_ref, ids_ref, router_ref), sems)
    width = hidden_ref.shape[1]
    experts = router_ref.shape[1]
    piece = min(width, PIECE)
    inv_rms = inv_rms_of(hidden_ref)
    logits = jnp.zeros((hidden_ref.shape[0], experts), jnp.float32)
    for i in range(width // piece):
        cols = pl.ds(i * piece, piece)
        normed = normed_piece(hidden_ref, gain_ref, inv_rms, cols)
        logits += jnp.dot(normed, router_ref[cols, :], preferred_element_type=jnp.float32)
    logits = logits.T
    raised = jnp.exp(logits - jnp.max(logits, axis=0, keepdims=True))
    probs = raised / jnp.sum(raised, axis=0, keepdims=True)
    ids = ids_ref[...]
    expert = lax.broadcasted_iota(jnp.int32, probs.shape, 0)
    picked = jnp.zeros(probs.shape, jnp.float32)
    for k in range(ids.shape[0]):
        picked = jnp.where(ids[k : k + 1] == expert, probs, picked)
    me = me_ref[0]
    named, place = slots_of(ids, me, flight)
    flying = jnp.concatenate(
        [
            jnp.sum(jnp.where(expert == (me ^ k), probs, 0.0), axis=0, keepdims=True)
            for k in range(flight)
        ],
        axis=0,
    )
    share = flying / jnp.sum(picked, axis=0, keepdims=True)
    weight = spread(named, place, share, flight).T
    high = weight.astype(jnp.bfloat16)
    low = (weight - high.astype(jnp.float32)).astype(jnp.bfloat16)
    out_ref[...] = jnp.concatenate([high, low], axis=1)


def expert_kernel(rows_ref, gate_ref, up_ref, down_ref, *refs):
    out_ref = refs[-1]
    rows = rows_ref[...]
    gate_act = jnp.dot(rows, gate_ref[0], preferred_element_type=jnp.float32)
    up_act = jnp.dot(rows, up_ref[0], preferred_element_type=jnp.float32)
    hidden_act = (jax.nn.silu(gate_act) * up_act).astype(jnp.bfloat16)
    width = out_ref.shape[1]
    piece = min(width, PIECE)
    for i in range(width // piece):
        cols = pl.ds(i * piece, piece)
        out_ref[:, cols] = jnp.dot(
            hidden_act, down_ref[0, :, cols], preferred_element_type=jnp.float32
        ).astype(jnp.bfloat16)


def expert_if_kernel(flag_ref, *refs):
    @pl.when(flag_ref[0] != 0)
    def _():
        expert_kernel(*refs)

    @pl.when(flag_ref[0] == 0)
    def _():
        refs[-1][...] = jnp.zeros_like(refs[-1])


def combine_kernel(weight_ref, *refs):
    *parts, out_ref, block_ref, sems = refs
    width = block_ref.shape[1]
    piece = min(width, COLUMNS)
    weight = weight_ref[...]
    copies = []
    for i in range(width // piece):
        cols = pl.ds(i * piece, piece)
        rows = jnp.concatenate([part[:, cols] for part in parts], axis=0)
        block_ref[:, cols] = jnp.dot(
            weight, jnp.concatenate([rows, rows], axis=0), preferred_element_type=jnp.float32
        ).astype(jnp.bfloat16)
        copy = pltpu.make_async_copy(block_ref.at[:, cols], out_ref.at[:, cols], sems.at[i])
        copy.start()
        copies.append(copy)
    for copy in copies:
        copy.wait()


def touch_kernel(*refs):
    refs[-1][...] = jnp.zeros_like(refs[-1])


def choose_kernel(flag_ref, ours_ref, theirs_ref, *refs):
    out_ref = refs[-1]

    @pl.when(flag_ref[0] != 0)
    def _():
        out_ref[...] = ours_ref[...]

    @pl.when(flag_ref[0] == 0)
    def _():
        out_ref[...] = theirs_ref[...]


def choose(flag, ours, theirs, after=()):
    return pl.pallas_call(
        choose_kernel,
        out_shape=jax.ShapeDtypeStruct(ours.shape, ours.dtype),
        in_specs=smem(1) + vmem(2) + anywhere(len(after)),
        out_specs=vmem(1)[0],
        compiler_params=params(),
        name="choose",
    )(flag, ours, theirs, *after)


def join_kernel(count, *refs):
    out_ref = refs[-1]
    depth = refs[0].shape[0]
    for at in range(count):
        out_ref[at * depth : (at + 1) * depth] = refs[at][...]


def join(parts, after=()):
    rows, width = parts[0].shape
    return pl.pallas_call(
        functools.partial(join_kernel, len(parts)),
        out_shape=jax.ShapeDtypeStruct((rows * len(parts), width), jnp.bfloat16),
        in_specs=vmem(len(parts)) + anywhere(len(after)),
        out_specs=vmem(1)[0],
        compiler_params=params(),
        name="join",
    )(*parts, *after)


def touch_any(*arrays):
    return pl.pallas_call(
        touch_kernel,
        out_shape=jax.ShapeDtypeStruct((8, 128), jnp.float32),
        in_specs=anywhere(len(arrays)),
        out_specs=vmem(1)[0],
        compiler_params=params(),
        name="seen",
    )(*arrays)


def mix_kernel(terms, *refs):
    out_refs = refs[terms[1] :]
    total = refs[0][...].astype(jnp.float32)
    for ref in refs[1 : terms[0]]:
        total = total + ref[...].astype(jnp.float32)
    depth = out_refs[0].shape[0]
    for at, out_ref in enumerate(out_refs):
        out_ref[...] = total[at * depth : (at + 1) * depth].astype(jnp.bfloat16)


def vmem(count):
    return [pl.BlockSpec(memory_space=pltpu.VMEM)] * count


def anywhere(count):
    return [pl.BlockSpec(memory_space=pl.ANY)] * count


def smem(count):
    return [pl.BlockSpec(memory_space=pltpu.SMEM)] * count


def params(limit=VMEM_LIMIT):
    return pltpu.CompilerParams(vmem_limit_bytes=limit)


def cost(flops, moved):
    return pl.CostEstimate(flops=flops, bytes_accessed=moved, transcendentals=0)


def dispatch(scalars, hidden, gain, ids, flight):
    return pl.pallas_call(
        functools.partial(dispatch_kernel, flight),
        out_shape=[jax.ShapeDtypeStruct((CAP, hidden.shape[1]), jnp.bfloat16)] * flight,
        in_specs=smem(len(scalars)) + anywhere(3),
        out_specs=vmem(flight),
        scratch_shapes=[pltpu.VMEM(x.shape, x.dtype) for x in (hidden, gain, ids)]
        + [pltpu.SemaphoreType.DMA((2 + PARTS,))],
        compiler_params=params(),
        cost_estimate=cost(hidden.size // 4, 128),
        name="dispatch",
    )(*scalars, hidden, gain, ids)


def shares(me, hidden, gain, ids, router, flight, *after):
    rows, width = hidden.shape
    return pl.pallas_call(
        functools.partial(shares_kernel, flight),
        out_shape=jax.ShapeDtypeStruct((rows, 2 * flight * CAP), jnp.bfloat16),
        in_specs=smem(1) + anywhere(4 + len(after)),
        out_specs=vmem(1)[0],
        scratch_shapes=[pltpu.VMEM(x.shape, x.dtype) for x in (hidden, gain, ids, router)]
        + [pltpu.SemaphoreType.DMA((4,))],
        compiler_params=params(),
        cost_estimate=cost(
            2 * hidden.size * router.shape[1], 2 * (hidden.size + router.size)
        ),
        name="shares",
    )(me, hidden, gain, ids, router, *after)


def touch(array, *after):
    return pl.pallas_call(
        touch_kernel,
        out_shape=jax.ShapeDtypeStruct((8, 128), jnp.float32),
        in_specs=vmem(1) + anywhere(len(after)),
        out_specs=vmem(1)[0],
        compiler_params=params(),
        name="touch",
    )(array, *after)


def mix(terms, pieces=1, after=()):
    rows, width = terms[0].shape
    shape = jax.ShapeDtypeStruct((rows // pieces, width), jnp.bfloat16)
    return pl.pallas_call(
        functools.partial(mix_kernel, (len(terms), len(terms) + len(after))),
        out_shape=[shape] * pieces,
        in_specs=vmem(len(terms)) + anywhere(len(after)),
        out_specs=vmem(pieces),
        compiler_params=params(),
        name="mix",
    )(*terms, *after)


def finish_kernel(count, flag_ref, own_ref, *refs):
    ours, theirs = refs[: count[0]], refs[count[0] : count[1]]
    out_refs = refs[count[2] :]
    depth = out_refs[0].shape[0]

    def add(others):
        total = own_ref[...].astype(jnp.float32)
        for ref in others:
            total = total + ref[...].astype(jnp.float32)
        for at, out_ref in enumerate(out_refs):
            out_ref[...] = total[at * depth : (at + 1) * depth].astype(jnp.bfloat16)

    @pl.when(flag_ref[0] != 0)
    def _():
        add(ours)

    @pl.when(flag_ref[0] == 0)
    def _():
        add(theirs)


def finish(flag, own, ours, theirs, pieces, after=()):
    rows, width = own.shape
    count = [len(ours), len(ours) + len(theirs), len(ours) + len(theirs) + len(after)]
    return pl.pallas_call(
        functools.partial(finish_kernel, count),
        out_shape=[jax.ShapeDtypeStruct((rows // pieces, width), jnp.bfloat16)] * pieces,
        in_specs=smem(1) + vmem(1 + count[1]) + anywhere(len(after)),
        out_specs=vmem(pieces),
        compiler_params=params(),
        name="finish",
    )(flag, own, *ours, *theirs, *after)


def expert(flag, rows, gate_weight, up_weight, down_weight, after=()):
    count = gate_weight.size + up_weight.size + down_weight.size
    flags = [] if flag is None else [flag]
    return pl.pallas_call(
        expert_kernel if flag is None else expert_if_kernel,
        out_shape=jax.ShapeDtypeStruct(rows.shape, jnp.bfloat16),
        in_specs=smem(len(flags)) + vmem(4) + anywhere(len(after)),
        out_specs=vmem(1)[0],
        compiler_params=params(),
        cost_estimate=cost(2 * rows.shape[0] * count, 2 * count),
        name="expert",
    )(*flags, rows, gate_weight, up_weight, down_weight, *after)


def combine(weight, parts):
    rows = weight.shape[0]
    width = parts[0].shape[1]
    return pl.pallas_call(
        combine_kernel,
        out_shape=jax.ShapeDtypeStruct((rows, width), jnp.bfloat16),
        in_specs=vmem(1 + len(parts)),
        out_specs=anywhere(1)[0],
        scratch_shapes=[
            pltpu.VMEM((rows, width), jnp.bfloat16),
            pltpu.SemaphoreType.DMA((width // min(width, COLUMNS),)),
        ],
        compiler_params=params(),
        name="combine",
    )(weight, *parts)


def in_plane(rows, k, flight):
    if k == 0:
        return rows
    pairs = [(m * flight + e, m * flight + (e ^ k)) for m in range(SPLIT) for e in range(flight)]
    with jax.named_scope("plane%d" % k):
        return lax.ppermute(rows, "expert", pairs)


def end_pair(rows, flight):
    pairs = [(m * flight + e, (m ^ 1) * flight + e) for m in range(SPLIT) for e in range(flight)]
    return lax.ppermute(rows, "expert", pairs)


def mirror_pair(rows, flight, members):
    pairs = [
        (m * flight + e, (SPLIT - 1 - m) * flight + e if m in members else m * flight + (e ^ 1))
        for m in range(SPLIT)
        for e in range(flight)
    ]
    return lax.ppermute(rows, "expert", pairs)


def inward_shift(rows, flight, near):
    to = {1: 0, 2: 3} if near else {1: 3, 2: 0}
    pairs = [(m * flight + e, to[m] * flight + e) for m in to for e in range(flight)]
    return lax.ppermute(rows, "expert", pairs)


def shards(hidden, norm_gain, router_weight, expert_ids, gate_weight, up_weight, down_weight):
    devices = lax.axis_size("expert")
    flight = devices // SPLIT
    gain = norm_gain.reshape(-1, 128)
    ids = expert_ids.T
    index = lax.axis_index("expert")
    member = lax.div(index, flight)
    me = lax.rem(index, flight).reshape(1)
    inner_number = lax.rem(lax.div(member + 1, 2), 2)
    at_inner, at_outer = inner_number.reshape(1), (1 - inner_number).reshape(1)
    half = flight // 2
    tick = []

    def then(value):
        tick[:] = [value[0] if isinstance(value, (list, tuple)) else value]
        return value

    def partial(rows, flag=None):
        return then(expert(flag, rows, gate_weight, up_weight, down_weight, tuple(tick)))

    def pick(ours, theirs):
        return then(choose(at_outer, ours, theirs, tuple(tick)))

    def total(*terms):
        return then(mix(terms, 1, tuple(tick)))[0]

    def seen(*arrays):
        return then(touch_any(*arrays, *tick))

    def end(name, rows):
        with jax.named_scope(name):
            return end_pair(rows, flight)

    def middle(name, rows, members=(1, 2)):
        with jax.named_scope(name):
            return mirror_pair(rows, flight, members)

    def inward(name, rows, near):
        with jax.named_scope(name):
            return inward_shift(rows, flight, near)

    hidden, gain, ids = (
        pltpu.with_memory_space_constraint(x, pltpu.HBM) for x in (hidden, gain, ids)
    )
    sent = then(dispatch((me, at_outer, at_inner), hidden, gain, ids, flight))
    came = [in_plane(rows, k, flight) for k, rows in enumerate(sent)]
    own_a = then(join(came[:half], tuple(tick)))
    near_a, far_in_a = end("near_a", own_a), middle("far_in_a", own_a)
    for array in (gate_weight, up_weight, down_weight):
        then(touch(array, *tick))
    own_b = then(join(came[half:], tuple(tick)))
    near_b, far_in_b = end("near_b", own_b), middle("far_in_b", own_b)
    near_part_a = partial(near_a)
    last_in_a = middle("last_in_a", near_a)
    two_a = end("two_a", pick(near_part_a, far_in_a))
    near_part_b = partial(near_b)
    two_b = end("two_b", pick(near_part_b, far_in_b))
    last_in_b = middle("last_in_b", near_b)
    seen(last_in_a)
    far_part_a = partial(pick(two_a, far_in_a))
    three_a = end("three_a", pick(far_part_a, last_in_a))
    across_b = middle("across_b", partial(last_in_b, at_inner))
    far_part_b = partial(pick(two_b, far_in_b))
    three_b = end("three_b", pick(far_part_b, last_in_b))
    mid_a = middle("mid_a", total(far_part_a, three_a))
    last_part_a = partial(pick(three_a, last_in_a))
    seen(across_b)
    four = end("four", pick(last_part_a, near_part_a))
    mid_b = middle("mid_b", total(far_part_b, three_b))
    sum_b = inward("sum_b", total(near_part_b, across_b), True)
    direct_b = middle("direct_b", partial(three_b, at_outer), (0, 3))
    seen(mid_a)
    across_a = inward("across_a", total(last_part_a, four), False)
    weight = then(shares(me, hidden, gain, ids, router_weight, flight, *tick))
    own_part_b, own_part_a = partial(own_b), partial(own_a)
    done_b = then(finish(at_outer, own_part_b, [sum_b, direct_b], [two_b, mid_b], half, tuple(tick)))
    done_a = then(finish(at_outer, own_part_a, [four, across_a], [two_a, mid_a], half, tuple(tick)))
    done = list(done_a) + list(done_b)
    back = [in_plane(rows, k, flight) for k, rows in enumerate(done)]
    return combine(weight, back)


def solution(mesh):
    tokens = P(("group", "expert"), None)
    sliced = P("expert", None, None)
    return jax.shard_map(
        shards,
        mesh=mesh,
        in_specs=(tokens, P(), P(), tokens, sliced, sliced, sliced),
        out_specs=tokens,
        check_vma=False,
    )
```
